32 devices in a mesh: dp: 16 (over z, x, core), batch: 2 (over y).
Axes of the slice: x: 2, y: 2, z: 4, core: 2. Of those that a mesh axis runs over, the one named last changes fastest.
Arguments:
- enc_input: bfloat16 [32, 1536, 512], P(('dp', 'batch')), may hold values from -6 to 6
- dec_input: bfloat16 [32, 1024, 512], P(('dp', 'batch')), may hold values from -6 to 6
- patch_counts: int32 [32, 4], P(('dp', 'batch')), may hold values from 1 to 1152, 1440 in all within a row
- table_lengths: int32 [32, 4], P(('dp', 'batch')), may hold values from 1 to 512, 960 in all within a row
- enc_qkv: bfloat16 [3, 512, 384], replicated, may hold values from -0.25 to 0.25
- enc_out_proj: bfloat16 [384, 512], replicated, may hold values from -2.5 to 2.5
- enc_gate_up: bfloat16 [2, 512, 1024], replicated, may hold values from -0.25 to 0.25
- enc_down: bfloat16 [1024, 512], replicated, may hold values from -0.1875 to 0.1875
- enc_gains: bfloat16 [2, 512], replicated, may hold values from 0.099609375 to 1.8984375
- dec_self_qkv: bfloat16 [3, 512, 384], replicated, may hold values from -0.25 to 0.25
- dec_self_out_proj: bfloat16 [384, 512], replicated, may hold values from -2.5 to 2.5
- dec_cross_qkv: bfloat16 [3, 512, 384], replicated, may hold values from -0.25 to 0.25
- dec_cross_out_proj: bfloat16 [384, 512], replicated, may hold values from -2.5 to 2.5
- dec_gate_up: bfloat16 [2, 512, 1024], replicated, may hold values from -0.25 to 0.25
- dec_down: bfloat16 [1024, 512], replicated, may hold values from -0.1875 to 0.1875
- dec_gains: bfloat16 [2, 512], replicated, may hold values from 0.099609375 to 1.8984375
- dec_ffn_gain: bfloat16 [512], replicated, may hold values from 0.099609375 to 1.8984375
- enc_cot: bfloat16 [32, 1536, 512], P(('dp', 'batch')), may hold values from -6 to 6
- dec_cot: bfloat16 [32, 1024, 512], P(('dp', 'batch')), may hold values from -6 to 6
Outputs:
- enc_output: bfloat16 [32, 1536, 512], P(('dp', 'batch'))
- dec_output: bfloat16 [32, 1024, 512], P(('dp', 'batch'))
- enc_input_grad: float32 [32, 1536, 512], P(('dp', 'batch'))
- dec_input_grad: float32 [32, 1024, 512], P(('dp', 'batch'))
- enc_qkv_grad: float32 [3, 512, 384], replicated
- enc_out_proj_grad: float32 [384, 512], replicated
- enc_gate_up_grad: float32 [2, 512, 1024], replicated
- enc_down_grad: float32 [1024, 512], replicated
- enc_gains_grad: float32 [2, 512], replicated
- dec_self_qkv_grad: float32 [3, 512, 384], replicated
- dec_self_out_proj_grad: float32 [384, 512], replicated
- dec_cross_qkv_grad: float32 [3, 512, 384], replicated
- dec_cross_out_proj_grad: float32 [384, 512], replicated
- dec_gate_up_grad: float32 [2, 512, 1024], replicated
- dec_down_grad: float32 [1024, 512], replicated
- dec_gains_grad: float32 [2, 512], replicated
- dec_ffn_gain_grad: float32 [512], replicated
The draws below stay inside these ranges and needn't reach their ends.
Inputs may be any that keep to these rules, and one draw needn't show every extreme that they name: `patch_counts`: each row's plots take 1536 - 1536 // 16 patch slots in all, in order from the row's start; the slots after them are padding. One plot of every row has exactly 1152 patches. `table_lengths`: each row's tables take 1024 - 1024 // 16 token slots in all, in the order of the plots; the slots after them are padding. One table of every row has exactly 512 tokens.
All inputs are finite; a program needn't handle non-finite values.
Results may differ from the reference program's by a relative error of at most 0.03.
The reference program's roundings to bfloat16 on the way count: a program that leaves them out, or rounds other values in their place, can miss the bound.
Values sent between devices are 32-bit elements; how exact they have to be, the bound alone decides.
No kernel may reach another device: no remote copies, remote signals or barrier semaphores. Data moves between devices by JAX's collectives and lax.ppermute only.
A program may use at most 256 MiB of HBM per device.

```python
import math
import jax
import jax.numpy as jnp
import numpy as np
from jax import lax

D = 512
HEADS = 6
HEAD_DIM = 64
FF = 1024
INNER = 384
ENC_LEN = 1536
DEC_LEN = 1024
PLOTS = 4
BLOCK = 512
ROWS = 32


def spiked(entries, own_key, source, target, shards_of, factor):
    def block_of(position):
        return (jnp.arange(entries.shape[position]) // (entries.shape[position] // shards_of)).reshape((-1,) + (1,) * (entries.ndim - 1 - position))

    one_side = jax.random.permutation(own_key, shards_of)[block_of(target)]
    far = (block_of(target) + shards_of // 2) % shards_of
    return jnp.where((block_of(source) == one_side) | (block_of(source) == far), factor * entries, entries)


def steps_of(key, shape, split, smallest, top_value):
    factor_of, own = 1.0, jax.random.fold_in(key, 6)
    for dim, parts in split:
        steps = jnp.exp(jax.random.uniform(jax.random.fold_in(own, dim), (parts,), jnp.float32, smallest / len(split), top_value / len(split)))
        factor_of = factor_of * jnp.repeat(steps, shape[dim] // parts).reshape([-1 if axis == dim else 1 for axis in range(len(shape))])
    return factor_of


def profile(count, total, bound, lean):
    weights = [(1 << 20) // math.isqrt(grade ** lean) + 1 for grade in range(2, count + 1)]
    rest, given = total - bound - (count - 1), [1] * (count - 1)
    while rest > 0:
        candidates = [i for i in range(count - 1) if given[i] < bound]
        pool, budget = sum([weights[i] for i in candidates]), rest
        for i in candidates:
            addition = min(bound - given[i], max(1, budget * weights[i] // pool), rest)
            given[i] = given[i] + addition
            rest = rest - addition
    return np.array([bound] + given)


def uneven_parts(key, count, total, bound, skew):
    if count == 2:
        one = jax.random.randint(key, (), max(1, total - bound), min(bound, total - 1) + 1)
        return jnp.stack([one, total - one])
    tallies = jnp.asarray(profile(count, total, bound, skew), jnp.int32)
    pairs = (count - 1) // 2
    giver, taker = tallies[1:1 + 2 * pairs:2], tallies[2:2 + 2 * pairs:2]
    slack = jnp.minimum(giver - 1, bound - taker)
    passed = jax.random.randint(jax.random.fold_in(key, 1), (pairs,), 0, 1 << 20) % (slack + 1)
    tallies = tallies.at[1:1 + 2 * pairs:2].set(giver - passed).at[2:2 + 2 * pairs:2].set(taker + passed)
    return tallies[jax.random.permutation(jax.random.fold_in(key, 2), count)]


def noise(stream_key, extent, width, limit, pieces=(), kind=jnp.bfloat16):
    factor_of = steps_of(stream_key, extent, pieces, -0.22, 0.18) if pieces else 1.0
    array = jax.random.normal(stream_key, extent, jnp.float32) * width * factor_of
    return jnp.minimum(jnp.maximum(array, -limit), limit).astype(kind)


def bell_draw_with(key, shape, width, bound, split, heavy, held_as=jnp.bfloat16):
    array = width * jax.random.normal(key, shape, jnp.float32)
    if split:
        array = array * steps_of(key, shape, split, -0.22, 0.18)
    return jnp.clip(spiked(array, jax.random.fold_in(key, 3), *heavy), -bound, bound).astype(held_as)


def setup_inputs(seed: int = 0) -> dict:
    splits = jax.random.split(jax.random.key(seed), 20)
    return {
        "enc_input": noise(splits[0], (ROWS, ENC_LEN, D), 1.0, 6.0, ((0, 32),)),
        "dec_input": noise(splits[1], (ROWS, DEC_LEN, D), 1.0, 6.0, ((0, 32),)),
        "patch_counts": jax.vmap(lambda own: uneven_parts(own, PLOTS, ENC_LEN - ENC_LEN // 16, ENC_LEN - ENC_LEN // 4, 2))(jax.random.split(splits[2], ROWS)).reshape((ROWS, PLOTS)).astype(jnp.int32),
        "table_lengths": jax.vmap(lambda own: uneven_parts(own, PLOTS, DEC_LEN - DEC_LEN // 16, DEC_LEN // 2, 1))(jax.random.split(splits[3], ROWS)).reshape((ROWS, PLOTS)).astype(jnp.int32),
        "enc_qkv": noise(splits[4], (3, D, INNER), D ** -0.5, 0.25),
        "enc_out_proj": noise(splits[5], (INNER, D), (INNER // 64) ** -0.5, 2.5),
        "enc_gate_up": noise(splits[6], (2, D, FF), D ** -0.5, 0.25),
        "enc_down": noise(splits[7], (FF, D), FF ** -0.5, 0.1875),
        "enc_gains": jnp.clip(1.0 + 0.18 * jax.random.normal(splits[8], (2, D), jnp.float32), 0.099609375, 1.8984375).astype(jnp.bfloat16),
        "dec_self_qkv": noise(splits[9], (3, D, INNER), D ** -0.5, 0.25),
        "dec_self_out_proj": noise(splits[10], (INNER, D), (INNER // 64) ** -0.5, 2.5),
        "dec_cross_qkv": noise(splits[11], (3, D, INNER), D ** -0.5, 0.25),
        "dec_cross_out_proj": noise(splits[12], (INNER, D), (INNER // 64) ** -0.5, 2.5),
        "dec_gate_up": noise(splits[13], (2, D, FF), D ** -0.5, 0.25),
        "dec_down": noise(splits[14], (FF, D), FF ** -0.5, 0.1875),
        "dec_gains": jnp.clip(1.0 + 0.18 * jax.random.normal(splits[15], (2, D), jnp.float32), 0.099609375, 1.8984375).astype(jnp.bfloat16),
        "dec_ffn_gain": jnp.clip(1.0 + 0.18 * jax.random.normal(splits[16], (D,), jnp.float32), 0.099609375, 1.8984375).astype(jnp.bfloat16),
        "enc_cot": bell_draw_with(splits[17], (ROWS, ENC_LEN, D), 1.0, 6.0, ((0, 32),), (0, 2, 32, 2.75)),
        "dec_cot": bell_draw_with(splits[18], (ROWS, DEC_LEN, D), 1.0, 6.0, ((0, 32),), (0, 2, 32, 2.75)),
    }


EPSILON = 1e-06
SCALE = 0.125
NEGATIVE = -1e+30
HIGH = lax.Precision.HIGHEST

@jax.custom_vjp
def low(v):
    return lax.optimization_barrier(v.astype(jnp.bfloat16)).astype(jnp.float32)

@jax.custom_vjp
def low_back(v):
    return v

def low_keep(v):
    return (low(v), None)

def low_pass(kept, grad):
    return (grad,)

def back_keep(v):
    return (v, None)

def back_low(kept, grad):
    return (low(grad),)
low.defvjp(low_keep, low_pass)
low_back.defvjp(back_keep, back_low)

def matmul_high(left, right):
    return jnp.dot(left, right, precision=HIGH)

def rms_norm(values, gain_vec):
    return values * lax.rsqrt(lax.optimization_barrier(jnp.mean(values * values, axis=-1, keepdims=True)) + EPSILON) * gain_vec

def segment_ids(counts, length):
    ends = jnp.cumsum(counts).astype(jnp.int32)
    places = jnp.arange(length, dtype=jnp.int32)
    return lax.optimization_barrier(jnp.sum((places[:, None] >= ends[None, :]).astype(jnp.int32), axis=1)).astype(jnp.int32)

def attention_high(query_rows, key_rows, value_rows, query_seg, key_seg, causal):
    length = query_rows.shape[0]
    blocks = length // BLOCK
    query_heads = query_rows.reshape(blocks, BLOCK, HEADS, HEAD_DIM)
    key_heads = key_rows.reshape(key_rows.shape[0], HEADS, HEAD_DIM)
    value_heads = value_rows.reshape(value_rows.shape[0], HEADS, HEAD_DIM)
    seg_blocks = query_seg.reshape(blocks, BLOCK)
    block_starts = jnp.arange(blocks, dtype=jnp.int32) * BLOCK
    key_places = jnp.arange(key_rows.shape[0], dtype=jnp.int32)

    @jax.checkpoint
    def one_block(block_args):
        query_block, seg_block, block_start = block_args
        scores = jnp.einsum('qhd,khd->hqk', query_block, key_heads, precision=HIGH) * SCALE
        allowed = seg_block[:, None] == key_seg[None, :]
        if causal:
            query_places = block_start + jnp.arange(BLOCK, dtype=jnp.int32)
            allowed = allowed & (query_places[:, None] >= key_places[None, :])
        scores = low_back(jnp.where(allowed[None], scores, NEGATIVE))
        attn_probs = low(jax.nn.softmax(scores, axis=-1))
        return jnp.einsum('hqk,khd->qhd', attn_probs, value_heads, precision=HIGH)
    attn_mixed = lax.map(one_block, (query_heads, seg_blocks, block_starts))
    return attn_mixed.reshape(length, HEADS * HEAD_DIM)

def attention_branch(normed, source, qkv_proj, out_proj, query_seg, key_seg, causal):
    query_rows = low(low_back(matmul_high(normed, qkv_proj[0])))
    key_rows = low(low_back(matmul_high(source, qkv_proj[1])))
    value_rows = low(low_back(matmul_high(source, qkv_proj[2])))
    attn_mixed = low(low_back(attention_high(query_rows, key_rows, value_rows, query_seg, key_seg, causal)))
    return low_back(matmul_high(attn_mixed, out_proj))

def ffn_branch(normed, gate_up, down_proj):
    gate_pre = low_back(matmul_high(normed, gate_up[0]))
    up_pre = low_back(matmul_high(normed, gate_up[1]))
    hidden = low(jax.nn.gelu(gate_pre, approximate=True) * up_pre)
    return low_back(matmul_high(hidden, down_proj))

def block_forward(enc_start, dec_start, params, enc_seg, dec_seg):
    enc_qkv, enc_out_proj, enc_gate_up, enc_down, enc_gains, dec_self_qkv, dec_self_out_proj, dec_cross_qkv, dec_cross_out_proj, dec_gate_up, dec_down, dec_gains, dec_ffn_gain = params
    normed = low(rms_norm(enc_start, enc_gains[0]))
    enc_mid = enc_start + attention_branch(normed, normed, enc_qkv, enc_out_proj, enc_seg, enc_seg, False)
    enc_sum = enc_mid + ffn_branch(low(rms_norm(enc_mid, enc_gains[1])), enc_gate_up, enc_down)
    memory = low(enc_sum)
    dec_normed = low(rms_norm(dec_start, dec_gains[0]))
    after_self = dec_start + attention_branch(dec_normed, dec_normed, dec_self_qkv, dec_self_out_proj, dec_seg, dec_seg, True)
    second = after_self + attention_branch(low(rms_norm(after_self, dec_gains[1])), memory, dec_cross_qkv, dec_cross_out_proj, dec_seg, enc_seg, False)
    dec_sum = second + ffn_branch(low(rms_norm(second, dec_ffn_gain)), dec_gate_up, dec_down)
    return (enc_sum, dec_sum)

def reference(enc_input, dec_input, patch_counts, table_lengths, enc_qkv, enc_out_proj, enc_gate_up, enc_down, enc_gains, dec_self_qkv, dec_self_out_proj, dec_cross_qkv, dec_cross_out_proj, dec_gate_up, dec_down, dec_gains, dec_ffn_gain, enc_cot, dec_cot):
    weights = tuple((weight_arg.astype(jnp.float32) for weight_arg in (enc_qkv, enc_out_proj, enc_gate_up, enc_down, enc_gains, dec_self_qkv, dec_self_out_proj, dec_cross_qkv, dec_cross_out_proj, dec_gate_up, dec_down, dec_gains, dec_ffn_gain)))

    def one_row(totals, row_data):
        enc_row, dec_row, counts, lengths, enc_cot_row, dec_cot_row = row_data
        enc_seg = segment_ids(counts, ENC_LEN)
        dec_seg = segment_ids(lengths, DEC_LEN)

        def forward(enc_start, dec_start, *params):
            return block_forward(enc_start, dec_start, params, enc_seg, dec_seg)
        outputs, pull_back = jax.vjp(forward, enc_row.astype(jnp.float32), dec_row.astype(jnp.float32), *weights)
        enc_keep = (enc_seg < PLOTS).astype(jnp.float32)[:, None]
        dec_keep = (dec_seg < PLOTS).astype(jnp.float32)[:, None]
        grad_list = pull_back((enc_cot_row.astype(jnp.float32) * enc_keep, dec_cot_row.astype(jnp.float32) * dec_keep))
        new_totals = tuple((total_grad + row_grad for total_grad, row_grad in zip(totals, grad_list[2:])))
        return (new_totals, (outputs[0].astype(jnp.bfloat16), outputs[1].astype(jnp.bfloat16), grad_list[0], grad_list[1]))
    zero_totals = tuple((jnp.zeros(weight_arg.shape, jnp.float32) for weight_arg in weights))
    totals, per_row = lax.scan(one_row, zero_totals, (enc_input, dec_input, patch_counts, table_lengths, enc_cot, dec_cot))
    return (per_row[0], per_row[1], per_row[2], per_row[3]) + tuple(totals)
```

```python
import functools

import jax
import jax.numpy as jnp
from jax import lax
from jax.experimental import pallas as pl
from jax.experimental.pallas import tpu as pltpu
from jax.sharding import PartitionSpec as P

BF = jnp.bfloat16
F32 = jnp.float32
EPS = 1e-06
NEG = -1e30
SCALE = 0.125
PLAIN = (((1,), (0,)), ((), ()))
NT = (((1,), (1,)), ((), ()))
TN = (((0,), (0,)), ((), ()))
AXES = ("dp", "batch")
GELU_C = 0.7978845608028654
GELU_A = 0.044715


def dot(a, b, dims=PLAIN):
    return lax.dot_general(a, b, dims, preferred_element_type=F32)


def bounds(counts):
    ends, total = [], 0
    for p in range(counts.shape[1]):
        total = total + counts[0, p]
        ends.append(total)
    return ends


def big_plot(counts, ends, size):
    index, start = jnp.int32(0), jnp.int32(0)
    for p in range(1, counts.shape[1]):
        hit = counts[0, p] == size
        index = jnp.where(hit, p, index)
        start = jnp.where(hit, ends[p - 1], start)
    return index, start


def segments(rotated, start, ends, length):
    slot = rotated + start
    slot = jnp.where(slot >= length, slot - length, slot)
    seg = jnp.zeros(rotated.shape, jnp.int32)
    for end in ends:
        seg = seg + (slot >= end).astype(jnp.int32)
    return seg


def iota(shape, dim):
    return lax.broadcasted_iota(jnp.int32, shape, dim)


def wrap(offset, length):
    return jnp.where(offset >= length, offset - length, offset)


def inverse_rms(x):
    return lax.rsqrt(jnp.mean(x * x, axis=1, keepdims=True) + EPS)


def norm_back(x, gain, grad):
    s = inverse_rms(x)
    xs = x * s
    gg = grad * gain
    inner = jnp.mean(gg * xs, axis=1, keepdims=True)
    return s * (gg - xs * inner), jnp.sum(grad * xs, axis=0, keepdims=True)


def fill_rotation(ring, source, length, extra, step=128):
    for r in range(0, length, step):
        ring[r : r + step, :] = source[r : r + step, :].astype(F32)
    ring[length : length + extra, :] = ring[0:extra, :]


def rotated_rows(ring, offset, count):
    base = pl.multiple_of((offset // 8) * 8, 8)
    sub = offset - base
    block = ring[pl.ds(base, count + 8), :]
    shape = (count // 8, 8, block.shape[1])
    turn = lax.rem(8 - sub, 8)
    first = pltpu.roll(block[0:count].reshape(shape), turn, 1)
    second = pltpu.roll(block[8 : count + 8].reshape(shape), turn, 1)
    return jnp.where(iota(shape, 1) < 8 - sub, first, second).reshape(count, shape[2])


def lanes_low(rows):
    return iota((rows, 128), 1) < 64


def head_of(x, low, h):
    zero = jnp.zeros_like(x)
    return jnp.where(low, x, zero) if h == 0 else jnp.where(low, zero, x)


def with_ones(v, low, h):
    one = jnp.ones_like(v)
    return jnp.where(low, v, one) if h == 0 else jnp.where(low, one, v)


def scores_of(qh, parts, sl):
    out = []
    for k, _, lo, hi, bias in parts:
        s = dot(qh, k[lo:hi, sl], NT)
        if bias is not None:
            s = s + bias()
        out.append(s)
    return out


def attend(q, rows, parts, mixed, lse, pairs):
    r0, r1 = rows
    low = lanes_low(r1 - r0)
    for pair in range(pairs):
        sl = slice(pair * 128, pair * 128 + 128)
        qp = q[r0:r1, sl]
        accs, tops = [], []
        for h in range(2):
            all_s = scores_of(head_of(qp, low, h), parts, sl)
            top = jnp.max(all_s[0], axis=1, keepdims=True)
            for s in all_s[1:]:
                top = jnp.maximum(top, jnp.max(s, axis=1, keepdims=True))
            acc = None
            for s, (_, v, lo, hi, _) in zip(all_s, parts):
                p = jnp.exp(s - top).astype(BF)
                term = dot(p, with_ones(v[lo:hi, sl], lanes_low(hi - lo), h))
                acc = term if acc is None else acc + term
            accs.append(acc)
            tops.append(top)
        total = pltpu.roll(jnp.where(low, accs[1], accs[0]), 64, 1)
        mixed[r0:r1, sl] = (jnp.where(low, accs[0], accs[1]) / total).astype(BF)
        lse[r0:r1, sl] = jnp.where(low, tops[0], tops[1]) + jnp.log(total)


def attend_back(q, qt, go, got, mixed, lse, rows, parts, dq, dkt, dvt, pairs):
    r0, r1 = rows
    low = lanes_low(r1 - r0)
    for pair in range(pairs):
        sl = slice(pair * 128, pair * 128 + 128)
        qp, gp = q[r0:r1, sl], go[r0:r1, sl]
        inner = gp.astype(F32) * mixed[r0:r1, sl].astype(F32)
        halves = []
        for h in range(2):
            hs = slice(pair * 128 + h * 64, pair * 128 + h * 64 + 64)
            qh, gh = head_of(qp, low, h), head_of(gp, low, h)
            delta = jnp.sum(head_of(inner, low, h), axis=1, keepdims=True)
            log_total = lse[r0:r1, hs.start : hs.start + 1]
            dq_h = None
            for s, (k, v, lo, hi, _) in zip(scores_of(qh, parts, sl), parts):
                p = jnp.exp(s - log_total)
                dp = dot(gh, v[lo:hi, sl], NT)
                ds = (p * (dp - delta)).astype(BF)
                dvt[hs, lo:hi] += dot(got[hs, r0:r1], p.astype(BF))
                dkt[hs, lo:hi] += dot(qt[hs, r0:r1], ds)
                term = dot(ds, k[lo:hi, sl])
                dq_h = term if dq_h is None else dq_h + term
            halves.append(dq_h)
        dq[r0:r1, sl] = (jnp.where(low, halves[0], halves[1]) * SCALE).astype(BF)


def gelu_parts(g):
    t = jnp.tanh(GELU_C * (g + GELU_A * g * g * g))
    return 0.5 * g * (1.0 + t), t


def project_rows(ring, start, length, step, gain, wq, wk, wv, xr, q, k, v):
    for r in range(0, length, step):
        x = rotated_rows(ring, wrap(r + start, length), step)
        xr[r : r + step, :] = x.astype(BF)
        n = (x * inverse_rms(x) * gain).astype(BF)
        q[r : r + step, :] = (dot(n, wq[...]).astype(BF) * SCALE).astype(BF)
        k[r : r + step, :] = dot(n, wk[...]).astype(BF)
        v[r : r + step, :] = dot(n, wv[...]).astype(BF)


def put_back(ring, start, length, extra, step, out):
    ring[length : length + extra, :] = ring[0:extra, :]
    for r in range(0, length, step):
        at = r - start
        at = jnp.where(at < 0, at + length, at)
        out[r : r + step, :] = rotated_rows(ring, at, step).astype(out.dtype)


def enc_forward_kernel(
    big, counts, x, qkv, wo, gu, wd, gains, out, memory, xr, q, k, v, mixed, lse, mid, ring, bias
):
    length = x.shape[0]
    rest = length - big
    step = rest
    ends = bounds(counts)
    _, start = big_plot(counts, ends, big)
    gain0 = gains[0:1, :].astype(F32)
    gain1 = gains[1:2, :].astype(F32)
    fill_rotation(ring, x, length, step + 8)
    project_rows(ring, start, length, step, gain0, qkv.at[0], qkv.at[1], qkv.at[2], xr, q, k, v)
    sq = segments(iota((rest, rest), 0) + big, start, ends, length)
    sk = segments(iota((rest, rest), 1) + big, start, ends, length)
    bias[...] = jnp.where(sq == sk, 0.0, NEG)
    pairs = q.shape[1] // 128
    for r in range(0, big, step):
        attend(q, (r, r + step), [(k, v, 0, big, None)], mixed, lse, pairs)
    attend(q, (big, length), [(k, v, big, length, lambda: bias[...])], mixed, lse, pairs)
    for r in range(0, length, step):
        rows = slice(r, r + step)
        m = xr[rows, :].astype(F32) + dot(mixed[rows, :], wo[...])
        mid[rows, :] = m
        n = (m * inverse_rms(m) * gain1).astype(BF)
        act, _ = gelu_parts(dot(n, gu[0]))
        hidden = (act * dot(n, gu[1])).astype(BF)
        total = m + dot(hidden, wd[...])
        ring[rows, :] = total
        memory[rows, :] = total.astype(BF)
    put_back(ring, start, length, step + 8, step, out)


def self_bias(bias, big, start, ends, length):
    shape = (big, big)
    row, col = iota(shape, 0), iota(shape, 1)
    bias[0, :, :] = jnp.where(row >= col, 0.0, NEG)
    same = segments(row + big, start, ends, length) == segments(col + big, start, ends, length)
    bias[1, :, :] = jnp.where(jnp.logical_and(row >= col, same), 0.0, NEG)


def self_tiles(big, bias, k, v):
    half = big // 2
    for b in range(2):
        at = b * big
        for t in range(2):
            lo, hi = t * half, (t + 1) * half
            part = (k, v, at, at + hi, lambda b=b, lo=lo, hi=hi: bias[b, lo:hi, 0:hi])
            yield (at + lo, at + hi), [part]


def cross_setup(ends_d, start_d, big_d, length_d, index_e, start_e, ends_e, big_e, length_e, bias):
    shape = (length_d - big_d, length_e - big_e)
    key = segments(iota(shape, 1) + big_e, start_e, ends_e, length_e)
    for b in range(2):
        query = segments(iota(shape, 0) + b * big_d, start_d, ends_d, length_d)
        bias[b, :, :] = jnp.where(query == key, 0.0, NEG)


def cross_run(same, big_d, length_d, big_e, length_e, rest_col, bias, k, v, run):
    first, second = (0, big_d), (big_d, length_d)
    whole = (k, v, 0, big_e, None)
    masked = (k, v, 0, big_e, rest_col)
    small0 = (k, v, big_e, length_e, lambda: bias[0])
    small1 = (k, v, big_e, length_e, lambda: bias[1])

    @pl.when(same)
    def _():
        run(first, [whole])
        run(second, [small1])

    @pl.when(jnp.logical_not(same))
    def _():
        run(first, [small0])
        run(second, [masked, small1])


def dec_forward_kernel(
    big_e, big_d,
    counts_e, counts_d, x, memory, qkv1, wo1, qkv2, wo2, gains,
    xr, q1, k1, v1, mixed1, lse1, after, q2, k2, v2, mixed2, lse2, second,
    ring, bias1, bias2,
):
    length = x.shape[0]
    length_e = memory.shape[0]
    step = big_d
    ends_d, ends_e = bounds(counts_d), bounds(counts_e)
    index_d, start_d = big_plot(counts_d, ends_d, big_d)
    index_e, start_e = big_plot(counts_e, ends_e, big_e)
    gain0 = gains[0:1, :].astype(F32)
    gain1 = gains[1:2, :].astype(F32)
    for r in range(0, length_e, 512):
        m = memory[r : r + 512, :]
        k2[r : r + 512, :] = dot(m, qkv2[1]).astype(BF)
        v2[r : r + 512, :] = dot(m, qkv2[2]).astype(BF)
    fill_rotation(ring, x, length, step + 8)
    project_rows(ring, start_d, length, step, gain0, qkv1.at[0], qkv1.at[1], qkv1.at[2], xr, q1, k1, v1)
    self_bias(bias1, big_d, start_d, ends_d, length)
    pairs = q1.shape[1] // 128
    for rows, parts in self_tiles(big_d, bias1, k1, v1):
        attend(q1, rows, parts, mixed1, lse1, pairs)
    for r in range(0, length, step):
        rows = slice(r, r + step)
        m = xr[rows, :].astype(F32) + dot(mixed1[rows, :], wo1[...])
        after[rows, :] = m
        n = (m * inverse_rms(m) * gain1).astype(BF)
        q2[rows, :] = (dot(n, qkv2[0]).astype(BF) * SCALE).astype(BF)
    cross_setup(ends_d, start_d, big_d, length, index_e, start_e, ends_e, big_e, length_e, bias2)
    seg_col = segments(iota((length - big_d, 1), 0) + big_d, start_d, ends_d, length)
    col = lambda: jnp.where(seg_col == index_e, 0.0, NEG)

    def run(rows, parts):
        attend(q2, rows, parts, mixed2, lse2, pairs)

    cross_run(index_d == index_e, big_d, length, big_e, length_e, col, bias2, k2, v2, run)
    for r in range(0, length, step):
        rows = slice(r, r + step)
        second[rows, :] = after[rows, :] + dot(mixed2[rows, :], wo2[...])


def ffn_back_rows(x, gain, gu, wd, r, n_buf, rb_buf, h_buf, dg_buf, du_buf, rows):
    n = (x * inverse_rms(x) * gain).astype(BF)
    g, u = dot(n, gu[0]), dot(n, gu[1])
    act, t = gelu_parts(g)
    h = (act * u).astype(BF)
    rb = r.astype(BF)
    gh = dot(rb, wd[...], NT)
    slope = 0.5 * (1.0 + t) + (0.5 * GELU_C) * g * (1.0 - t * t) * (1.0 + (3.0 * GELU_A) * g * g)
    dg = (gh * u * slope).astype(BF)
    du = (gh * act).astype(BF)
    n_buf[rows, :] = n
    rb_buf[rows, :] = rb
    h_buf[rows, :] = h
    dg_buf[rows, :] = dg
    du_buf[rows, :] = du
    return h, dot(dg, gu[0], NT) + dot(du, gu[1], NT)


def ffn_weight_grads(n_buf, rb_buf, h_buf, dg_buf, du_buf, d_gu, d_down):
    d_down[...] = dot(h_buf[...], rb_buf[...], TN)
    d_gu[0, :, :] = dot(n_buf[...], dg_buf[...], TN)
    d_gu[1, :, :] = dot(n_buf[...], du_buf[...], TN)


def row_mask(start, ends, length, r, step):
    slot = wrap(iota((step, 1), 0) + r + start, length)
    return slot < ends[-1]


def dec_ffn_kernel(
    big_d, counts_d, second, cot, gu, wd, gain,
    out, grad_second, d_gu, d_down, d_gain,
    ring, n_buf, rb_buf, h_buf, dg_buf, du_buf,
):
    length = second.shape[0]
    step = big_d
    ends = bounds(counts_d)
    _, start = big_plot(counts_d, ends, big_d)
    gain_row = gain[0:1, :].astype(F32)
    fill_rotation(ring, cot, length, step + 8)
    for r in range(0, length, step):
        rows = slice(r, r + step)
        c = rotated_rows(ring, wrap(r + start, length), step)
        grad_second[rows, :] = jnp.where(row_mask(start, ends, length, r, step), c, 0.0)
    total = None
    for r in range(0, length, step):
        rows = slice(r, r + step)
        x = second[rows, :]
        c = grad_second[rows, :]
        h, gn = ffn_back_rows(x, gain_row, gu, wd, c, n_buf, rb_buf, h_buf, dg_buf, du_buf, rows)
        ring[rows, :] = x + dot(h, wd[...])
        gx, gg = norm_back(x, gain_row, gn)
        grad_second[rows, :] = c + gx
        total = gg if total is None else total + gg
    d_gain[...] = total
    ffn_weight_grads(n_buf, rb_buf, h_buf, dg_buf, du_buf, d_gu, d_down)
    put_back(ring, start, length, step + 8, step, out)


def enc_ffn_kernel(
    big_e, counts_e, mid, cot, grad_memory, gu, wd, gains,
    grad_mid, d_gu, d_down, d_gain,
    ring, n_buf, rb_buf, h_buf, dg_buf, du_buf,
):
    length = mid.shape[0]
    step = length - big_e
    ends = bounds(counts_e)
    _, start = big_plot(counts_e, ends, big_e)
    gain_row = gains[1:2, :].astype(F32)
    fill_rotation(ring, cot, length, step + 8)
    total = None
    for r in range(0, length, step):
        rows = slice(r, r + step)
        c = rotated_rows(ring, wrap(r + start, length), step)
        c = jnp.where(row_mask(start, ends, length, r, step), c, 0.0) + grad_memory[rows, :]
        x = mid[rows, :]
        _, gn = ffn_back_rows(x, gain_row, gu, wd, c, n_buf, rb_buf, h_buf, dg_buf, du_buf, rows)
        gx, gg = norm_back(x, gain_row, gn)
        grad_mid[rows, :] = c + gx
        total = gg if total is None else total + gg
    d_gain[...] = total
    ffn_weight_grads(n_buf, rb_buf, h_buf, dg_buf, du_buf, d_gu, d_down)


def mixed_grads(r, wo, mixed, rb, go, got, d_wo, step):
    for at in range(0, r.shape[0], step):
        rows = slice(at, at + step)
        b = r[rows, :].astype(BF)
        rb[rows, :] = b
        g = dot(b, wo[...], NT).astype(BF)
        go[rows, :] = g
        got[:, rows] = g.T
    d_wo[...] = dot(mixed[...], rb[...], TN)


def cross_back_kernel(
    big_e, big_d,
    counts_e, counts_d, grad_second, after, memory, q, k, v, mixed, lse, qkv, wo, gains,
    grad_first, grad_memory, d_qkv, d_wo, d_gain,
    rb, go, got, qt, dq, dkt, dvt, dk, dv, n_buf, bias,
):
    length, length_e = after.shape[0], memory.shape[0]
    step = big_d
    ends_d, ends_e = bounds(counts_d), bounds(counts_e)
    index_d, start_d = big_plot(counts_d, ends_d, big_d)
    index_e, start_e = big_plot(counts_e, ends_e, big_e)
    gain_row = gains[1:2, :].astype(F32)
    mixed_grads(grad_second, wo, mixed, rb, go, got, d_wo, step)
    for r in range(0, length, step):
        qt[:, r : r + step] = q[r : r + step, :].T
    dkt[...] = jnp.zeros_like(dkt)
    dvt[...] = jnp.zeros_like(dvt)
    cross_setup(ends_d, start_d, big_d, length, index_e, start_e, ends_e, big_e, length_e, bias)
    seg_col = segments(iota((length - big_d, 1), 0) + big_d, start_d, ends_d, length)
    col = lambda: jnp.where(seg_col == index_e, 0.0, NEG)
    pairs = q.shape[1] // 128

    def run(rows, parts):
        attend_back(q, qt, go, got, mixed, lse, rows, parts, dq, dkt, dvt, pairs)

    cross_run(index_d == index_e, big_d, length, big_e, length_e, col, bias, k, v, run)
    for r in range(0, length_e, 512):
        cols = slice(r, r + 512)
        dk[cols, :] = dkt[:, cols].T.astype(BF)
        dv[cols, :] = dvt[:, cols].T.astype(BF)
        grad_memory[cols, :] = dot(dk[cols, :], qkv[1], NT) + dot(dv[cols, :], qkv[2], NT)
    total = None
    for r in range(0, length, step):
        rows = slice(r, r + step)
        x = after[rows, :]
        n_buf[rows, :] = (x * inverse_rms(x) * gain_row).astype(BF)
        gx, gg = norm_back(x, gain_row, dot(dq[rows, :], qkv[0], NT))
        grad_first[rows, :] = grad_second[rows, :] + gx
        total = gg if total is None else total + gg
    d_gain[...] = total
    d_qkv[0, :, :] = dot(n_buf[...], dq[...], TN)
    d_qkv[1, :, :] = dot(memory[...], dk[...], TN)
    d_qkv[2, :, :] = dot(memory[...], dv[...], TN)


def self_back_tail(
    length, step, grad, xr, qkv, gain_row, start, dq, dkt, dvt, dk, dv, n_buf, ring, d_qkv, d_gain, out
):
    total = None
    for r in range(0, length, step):
        rows = slice(r, r + step)
        dk[rows, :] = dkt[:, rows].T.astype(BF)
        dv[rows, :] = dvt[:, rows].T.astype(BF)
        x = xr[rows, :].astype(F32)
        n_buf[rows, :] = (x * inverse_rms(x) * gain_row).astype(BF)
        gn = dot(dq[rows, :], qkv[0], NT) + dot(dk[rows, :], qkv[1], NT) + dot(dv[rows, :], qkv[2], NT)
        gx, gg = norm_back(x, gain_row, gn)
        ring[rows, :] = grad[rows, :] + gx
        total = gg if total is None else total + gg
    d_gain[...] = total
    d_qkv[0, :, :] = dot(n_buf[...], dq[...], TN)
    d_qkv[1, :, :] = dot(n_buf[...], dk[...], TN)
    d_qkv[2, :, :] = dot(n_buf[...], dv[...], TN)
    put_back(ring, start, length, step + 8, step, out)


def dec_self_back_kernel(
    big_d,
    counts_d, grad_first, xr, q, k, v, mixed, lse, qkv, wo, gains,
    out, d_qkv, d_wo, d_gain,
    ring, rb, go, got, qt, dq, dkt, dvt, dk, dv, n_buf, bias,
):
    length = xr.shape[0]
    step = big_d
    ends = bounds(counts_d)
    _, start = big_plot(counts_d, ends, big_d)
    gain_row = gains[0:1, :].astype(F32)
    mixed_grads(grad_first, wo, mixed, rb, go, got, d_wo, step)
    for r in range(0, length, step):
        qt[:, r : r + step] = q[r : r + step, :].T
    dkt[...] = jnp.zeros_like(dkt)
    dvt[...] = jnp.zeros_like(dvt)
    self_bias(bias, big_d, start, ends, length)
    for rows, parts in self_tiles(big_d, bias, k, v):
        attend_back(q, qt, go, got, mixed, lse, rows, parts, dq, dkt, dvt, q.shape[1] // 128)
    self_back_tail(
        length, step, grad_first, xr, qkv, gain_row, start, dq, dkt, dvt, dk, dv, n_buf, ring, d_qkv, d_gain, out
    )


def enc_self_back_kernel(
    big_e,
    counts_e, grad_mid, xr, q, k, v, mixed, lse, qkv, wo, gains,
    out, d_qkv, d_wo, d_gain,
    ring, rb, go, got, qt, dq, dkt, dvt, dk, dv, n_buf, bias,
):
    length = xr.shape[0]
    rest = length - big_e
    step = rest
    ends = bounds(counts_e)
    _, start = big_plot(counts_e, ends, big_e)
    gain_row = gains[0:1, :].astype(F32)
    mixed_grads(grad_mid, wo, mixed, rb, go, got, d_wo, step)
    for r in range(0, length, step):
        qt[:, r : r + step] = q[r : r + step, :].T
    dkt[...] = jnp.zeros_like(dkt)
    dvt[...] = jnp.zeros_like(dvt)
    sq = segments(iota((rest, rest), 0) + big_e, start, ends, length)
    sk = segments(iota((rest, rest), 1) + big_e, start, ends, length)
    bias[...] = jnp.where(sq == sk, 0.0, NEG)
    pairs = q.shape[1] // 128
    for r in range(0, big_e, step):
        attend_back(q, qt, go, got, mixed, lse, (r, r + step), [(k, v, 0, big_e, None)], dq, dkt, dvt, pairs)
    parts = [(k, v, big_e, length, lambda: bias[...])]
    attend_back(q, qt, go, got, mixed, lse, (big_e, length), parts, dq, dkt, dvt, pairs)
    self_back_tail(
        length, step, grad_mid, xr, qkv, gain_row, start, dq, dkt, dvt, dk, dv, n_buf, ring, d_qkv, d_gain, out
    )


def call(kernel, name, scalars, arrays, outs, scratch, flops):
    vmem = pl.BlockSpec(memory_space=pltpu.VMEM)
    smem = pl.BlockSpec(memory_space=pltpu.SMEM)
    size = sum(a.size * a.dtype.itemsize for a in arrays)
    size += sum(o.size * o.dtype.itemsize for o in outs)
    return pl.pallas_call(
        kernel,
        out_shape=tuple(outs),
        in_specs=[smem] * len(scalars) + [vmem] * len(arrays),
        out_specs=tuple([vmem] * len(outs)),
        scratch_shapes=[pltpu.VMEM(s, d) for s, d in scratch],
        compiler_params=pltpu.CompilerParams(vmem_limit_bytes=VMEM_LIMIT),
        cost_estimate=pl.CostEstimate(flops=flops, bytes_accessed=size, transcendentals=0),
        name=name,
    )(*scalars, *arrays)


VMEM_LIMIT = 58 << 20


def like(shape, dtype):
    return jax.ShapeDtypeStruct(shape, dtype)


def one_row(enc_row, dec_row, counts, lengths, enc_w, dec_w, enc_cot, dec_cot):
    enc_qkv, enc_wo, enc_gu, enc_wd, enc_gains = enc_w
    self_qkv, self_wo, cross_qkv, cross_wo, dec_gu, dec_wd, dec_gains, dec_gain = dec_w
    le, width = enc_row.shape
    ld = dec_row.shape[0]
    inner = enc_wo.shape[0]
    ff = enc_wd.shape[0]
    big_e, big_d = le - le // 4, ld // 2
    rest_e = le - big_e

    out_e, memory, xr_e, q_e, k_e, v_e, mixed_e, lse_e, mid = call(
        functools.partial(enc_forward_kernel, big_e), "enc_forward",
        [counts], [enc_row, enc_qkv, enc_wo, enc_gu, enc_wd, enc_gains],
        [like((le, width), BF)] * 3 + [like((le, inner), BF)] * 4 + [like((le, inner), F32), like((le, width), F32)],
        [((le + rest_e + 8, width), F32), ((rest_e, rest_e), F32)], 11_000_000_000,
    )
    xr_d, q1, k1, v1, mixed1, lse1, after, q2, k2, v2, mixed2, lse2, second = call(
        functools.partial(dec_forward_kernel, big_e, big_d), "dec_forward",
        [counts, lengths], [dec_row, memory, self_qkv, self_wo, cross_qkv, cross_wo, dec_gains],
        [like((ld, width), BF)] + [like((ld, inner), BF)] * 4 + [like((ld, inner), F32), like((ld, width), F32)]
        + [like((ld, inner), BF), like((le, inner), BF), like((le, inner), BF), like((ld, inner), BF)]
        + [like((ld, inner), F32), like((ld, width), F32)],
        [((ld + big_d + 8, width), F32), ((2, big_d, big_d), F32), ((2, ld - big_d, rest_e), F32)], 8_000_000_000,
    )

    def ffn_scratch(length, extra):
        return [((length + extra + 8, width), F32), ((length, width), BF), ((length, width), BF)] + [((length, ff), BF)] * 3

    ffn_grads = [like((2, width, ff), F32), like((ff, width), F32), like((1, width), F32)]
    out_d, grad_second, d_dec_gu, d_dec_wd, d_gain3 = call(
        functools.partial(dec_ffn_kernel, big_d), "dec_ffn",
        [lengths], [second, dec_cot, dec_gu, dec_wd, dec_gain.reshape(1, width)],
        [like((ld, width), BF), like((ld, width), F32)] + ffn_grads,
        ffn_scratch(ld, big_d), 10_000_000_000,
    )

    def attn_scratch(lq, lk):
        return [
            ((lq, width), BF), ((lq, inner), BF), ((inner, lq), BF), ((inner, lq), BF), ((lq, inner), BF),
            ((inner, lk), F32), ((inner, lk), F32), ((lk, inner), BF), ((lk, inner), BF), ((lq, width), BF),
        ]

    attn_grads = [like((3, width, inner), F32), like((inner, width), F32), like((1, width), F32)]
    grad_first, grad_memory, d_cross_qkv, d_cross_wo, d_gain2 = call(
        functools.partial(cross_back_kernel, big_e, big_d), "cross_back",
        [counts, lengths], [grad_second, after, memory, q2, k2, v2, mixed2, lse2, cross_qkv, cross_wo, dec_gains],
        [like((ld, width), F32), like((le, width), F32)] + attn_grads,
        attn_scratch(ld, le) + [((2, ld - big_d, rest_e), F32)], 14_000_000_000,
    )
    grad_mid, d_enc_gu, d_enc_wd, d_enc_gain2 = call(
        functools.partial(enc_ffn_kernel, big_e), "enc_ffn",
        [counts], [mid, enc_cot, grad_memory, enc_gu, enc_wd, enc_gains],
        [like((le, width), F32)] + ffn_grads,
        ffn_scratch(le, rest_e), 14_000_000_000,
    )
    grad_dec, d_self_qkv, d_self_wo, d_gain1 = call(
        functools.partial(dec_self_back_kernel, big_d), "dec_self_back",
        [lengths], [grad_first, xr_d, q1, k1, v1, mixed1, lse1, self_qkv, self_wo, dec_gains],
        [like((ld, width), F32)] + attn_grads,
        [((ld + big_d + 8, width), F32)] + attn_scratch(ld, ld) + [((2, big_d, big_d), F32)], 8_000_000_000,
    )
    grad_enc, d_enc_qkv, d_enc_wo, d_enc_gain1 = call(
        functools.partial(enc_self_back_kernel, big_e), "enc_self_back",
        [counts], [grad_mid, xr_e, q_e, k_e, v_e, mixed_e, lse_e, enc_qkv, enc_wo, enc_gains],
        [like((le, width), F32)] + attn_grads,
        [((le + rest_e + 8, width), F32)] + attn_scratch(le, le) + [((rest_e, rest_e), F32)], 18_000_000_000,
    )
    grads = (
        d_enc_qkv, d_enc_wo, d_enc_gu, d_enc_wd, jnp.concatenate([d_enc_gain1, d_enc_gain2]),
        d_self_qkv, d_self_wo, d_cross_qkv, d_cross_wo, d_dec_gu, d_dec_wd,
        jnp.concatenate([d_gain1, d_gain2]), d_gain3.reshape(width),
    )
    return (out_e, out_d, grad_enc, grad_dec), grads


def shards(enc_input, dec_input, patch_counts, table_lengths, *rest):
    enc_w, dec_w, (enc_cot, dec_cot) = rest[:5], rest[5:13], rest[13:]
    outs, totals = [], None
    for b in range(enc_input.shape[0]):
        row, grads = one_row(
            enc_input[b], dec_input[b], patch_counts[b : b + 1], table_lengths[b : b + 1],
            enc_w, dec_w, enc_cot[b], dec_cot[b],
        )
        outs.append(row)
        totals = grads if totals is None else tuple(a + g for a, g in zip(totals, grads))
    placed = tuple(jnp.stack([row[i] for row in outs]) for i in range(4))
    return placed + tuple(lax.psum(totals, AXES))


def solution(mesh):
    rows3 = P(AXES, None, None)
    rows2 = P(AXES, None)
    return jax.shard_map(
        shards,
        mesh=mesh,
        in_specs=(rows3, rows3, rows2, rows2) + (P(),) * 13 + (rows3, rows3),
        out_specs=(rows3,) * 4 + (P(),) * 13,
        check_vma=False,
    )
```

```python
import functools

import jax
import jax.numpy as jnp
from jax import lax
from jax.experimental import pallas as pl
from jax.experimental.pallas import tpu as pltpu
from jax.sharding import PartitionSpec as P

BF = jnp.bfloat16
F32 = jnp.float32
EPS = 1e-06
NEG = -1e30
SCALE = 0.125
PLAIN = (((1,), (0,)), ((), ()))
NT = (((1,), (1,)), ((), ()))
TN = (((0,), (0,)), ((), ()))
AXES = ("dp", "batch")
GELU_C = 0.7978845608028654
GELU_A = 0.044715
EXTRA = 24


def dot(a, b, dims=PLAIN):
    return lax.dot_general(a, b, dims, preferred_element_type=F32)


def bounds(counts):
    ends, total = [], 0
    for p in range(counts.shape[1]):
        total = total + counts[0, p]
        ends.append(total)
    return ends


def big_plot(counts, ends, size):
    index, start = jnp.int32(0), jnp.int32(0)
    for p in range(1, counts.shape[1]):
        hit = counts[0, p] == size
        index = jnp.where(hit, p, index)
        start = jnp.where(hit, ends[p - 1], start)
    return index, start


def segments(rotated, start, ends, length):
    slot = rotated + start
    slot = jnp.where(slot >= length, slot - length, slot)
    seg = jnp.zeros(rotated.shape, jnp.int32)
    for end in ends:
        seg = seg + (slot >= end).astype(jnp.int32)
    return seg


def iota(shape, dim):
    return lax.broadcasted_iota(jnp.int32, shape, dim)


def wrap(offset, length):
    return jnp.where(offset >= length, offset - length, offset)


def inverse_rms(x):
    return lax.rsqrt(jnp.mean(x * x, axis=1, keepdims=True) + EPS)


def norm_back(x, gain, grad):
    s = inverse_rms(x)
    xs = x * s
    gg = grad * gain
    inner = jnp.mean(gg * xs, axis=1, keepdims=True)
    return s * (gg - xs * inner), jnp.sum(grad * xs, axis=0, keepdims=True)


def fill_rotation(ring, source, length, extra, step=128):
    for r in range(0, length, step):
        ring[r : r + step, :] = source[r : r + step, :].astype(F32)
    ring[length : length + extra, :] = ring[0:extra, :]


def rotated_rows(ring, offset, count):
    base = pl.multiple_of((offset // 8) * 8, 8)
    sub = offset - base
    block = ring[pl.ds(base, count + 8), :]
    shape = (count // 8, 8, block.shape[1])
    turn = lax.rem(8 - sub, 8)
    first = pltpu.roll(block[0:count].reshape(shape), turn, 1)
    second = pltpu.roll(block[8 : count + 8].reshape(shape), turn, 1)
    return jnp.where(iota(shape, 1) < 8 - sub, first, second).reshape(count, shape[2])


def lanes_low(rows):
    return iota((rows, 128), 1) < 64


def head_of(x, low, h):
    zero = jnp.zeros_like(x)
    return jnp.where(low, x, zero) if h == 0 else jnp.where(low, zero, x)


def with_ones(v, low, h):
    one = jnp.ones_like(v)
    return jnp.where(low, v, one) if h == 0 else jnp.where(low, one, v)


def scores_of(qh, parts, sl):
    out = []
    for k, _, lo, hi, bias in parts:
        s = dot(qh, k[lo:hi, sl], NT)
        if bias is not None:
            s = s + bias()
        out.append(s)
    return out


def attend(q, rows, parts, mixed, lse, pairs):
    r0, r1 = rows
    low = lanes_low(r1 - r0)
    for pair in range(pairs):
        sl = slice(pair * 128, pair * 128 + 128)
        qp = q[r0:r1, sl]
        accs, tops = [], []
        for h in range(2):
            all_s = scores_of(head_of(qp, low, h), parts, sl)
            top = jnp.max(all_s[0], axis=1, keepdims=True)
            for s in all_s[1:]:
                top = jnp.maximum(top, jnp.max(s, axis=1, keepdims=True))
            acc = None
            for s, (_, v, lo, hi, _) in zip(all_s, parts):
                p = jnp.exp(s - top).astype(BF)
                term = dot(p, with_ones(v[lo:hi, sl], lanes_low(hi - lo), h))
                acc = term if acc is None else acc + term
            accs.append(acc)
            tops.append(top)
        total = pltpu.roll(jnp.where(low, accs[1], accs[0]), 64, 1)
        mixed[r0:r1, sl] = (jnp.where(low, accs[0], accs[1]) / total).astype(BF)
        lse[r0:r1, sl] = jnp.where(low, tops[0], tops[1]) + jnp.log(total)


def attend_back(q, qt, go, got, mixed, lse, rows, parts, dq, dkt, dvt, pairs):
    r0, r1 = rows
    low = lanes_low(r1 - r0)
    for pair in range(pairs):
        sl = slice(pair * 128, pair * 128 + 128)
        qp, gp = q[r0:r1, sl], go[r0:r1, sl]
        inner = gp.astype(F32) * mixed[r0:r1, sl].astype(F32)
        halves = []
        for h in range(2):
            hs = slice(pair * 128 + h * 64, pair * 128 + h * 64 + 64)
            qh, gh = head_of(qp, low, h), head_of(gp, low, h)
            delta = jnp.sum(head_of(inner, low, h), axis=1, keepdims=True)
            log_total = lse[r0:r1, hs.start : hs.start + 1]
            dq_h = None
            for s, (k, v, lo, hi, _) in zip(scores_of(qh, parts, sl), parts):
                p = jnp.exp(s - log_total)
                dp = dot(gh, v[lo:hi, sl], NT)
                ds = (p * (dp - delta)).astype(BF)
                dvt[hs, lo:hi] += dot(got[hs, r0:r1], p.astype(BF))
                dkt[hs, lo:hi] += dot(qt[hs, r0:r1], ds)
                term = dot(ds, k[lo:hi, sl])
                dq_h = term if dq_h is None else dq_h + term
            halves.append(dq_h)
        dq[r0:r1, sl] = (jnp.where(low, halves[0], halves[1]) * SCALE).astype(BF)


def gelu_parts(g):
    t = jnp.tanh(GELU_C * (g + GELU_A * g * g * g))
    return 0.5 * g * (1.0 + t), t


def project_rows(ring, start, length, step, gain, wq, wk, wv, xr, q, k, v):
    for r in range(0, length, step):
        x = rotated_rows(ring, wrap(r + start, length), step)
        xr[r : r + step, :] = x.astype(BF)
        n = (x * inverse_rms(x) * gain).astype(BF)
        q[r : r + step, :] = (dot(n, wq[...]).astype(BF) * SCALE).astype(BF)
        k[r : r + step, :] = dot(n, wk[...]).astype(BF)
        v[r : r + step, :] = dot(n, wv[...]).astype(BF)


def put_back(ring, start, length, extra, step, out):
    ring[length : length + extra, :] = ring[0:extra, :]
    for r in range(0, length, step):
        at = r - start
        at = jnp.where(at < 0, at + length, at)
        out[r : r + step, :] = rotated_rows(ring, at, step).astype(out.dtype)


def enc_forward_kernel(
    big, counts, x, qkv, wo, gu, wd, gains, out, memory, xr, q, k, v, mixed, lse, mid, ring, bias
):
    length = x.shape[0]
    rest = length - big
    step = rest
    ends = bounds(counts)
    _, start = big_plot(counts, ends, big)
    gain0 = gains[0:1, :].astype(F32)
    gain1 = gains[1:2, :].astype(F32)
    fill_rotation(ring, x, length, step + 8)
    project_rows(ring, start, length, step, gain0, qkv.at[0], qkv.at[1], qkv.at[2], xr, q, k, v)
    sq = segments(iota((rest, rest), 0) + big, start, ends, length)
    sk = segments(iota((rest, rest), 1) + big, start, ends, length)
    bias[...] = jnp.where(sq == sk, 0.0, NEG)
    pairs = q.shape[1] // 128
    for r in range(0, big, step):
        attend(q, (r, r + step), [(k, v, 0, big, None)], mixed, lse, pairs)
    attend(q, (big, length), [(k, v, big, length, lambda: bias[...])], mixed, lse, pairs)
    for r in range(0, length, step):
        rows = slice(r, r + step)
        m = xr[rows, :].astype(F32) + dot(mixed[rows, :], wo[...])
        mid[rows, :] = m
        n = (m * inverse_rms(m) * gain1).astype(BF)
        act, _ = gelu_parts(dot(n, gu[0]))
        hidden = (act * dot(n, gu[1])).astype(BF)
        total = m + dot(hidden, wd[...])
        ring[rows, :] = total
        memory[rows, :] = total.astype(BF)
    put_back(ring, start, length, step + 8, step, out)


def self_bias(bias, big, start, ends, length):
    shape = (big, big)
    row, col = iota(shape, 0), iota(shape, 1)
    bias[0, :, :] = jnp.where(row >= col, 0.0, NEG)
    same = segments(row + big, start, ends, length) == segments(col + big, start, ends, length)
    bias[1, :, :] = jnp.where(jnp.logical_and(row >= col, same), 0.0, NEG)


def self_tiles(big, bias, k, v):
    half = big // 2
    for b in range(2):
        at = b * big
        for t in range(2):
            lo, hi = t * half, (t + 1) * half
            part = (k, v, at, at + hi, lambda b=b, lo=lo, hi=hi: bias[b, lo:hi, 0:hi])
            yield (at + lo, at + hi), [part]


def cross_setup(ends_d, start_d, big_d, length_d, index_e, start_e, ends_e, big_e, length_e, bias):
    shape = (length_d - big_d, length_e - big_e)
    key = segments(iota(shape, 1) + big_e, start_e, ends_e, length_e)
    for b in range(2):
        query = segments(iota(shape, 0) + b * big_d, start_d, ends_d, length_d)
        bias[b, :, :] = jnp.where(query == key, 0.0, NEG)


def cross_run(same, big_d, length_d, big_e, length_e, rest_col, bias, k, v, run):
    first, second = (0, big_d), (big_d, length_d)
    whole = (k, v, 0, big_e, None)
    masked = (k, v, 0, big_e, rest_col)
    small0 = (k, v, big_e, length_e, lambda: bias[0])
    small1 = (k, v, big_e, length_e, lambda: bias[1])

    @pl.when(same)
    def _():
        run(first, [whole])
        run(second, [small1])

    @pl.when(jnp.logical_not(same))
    def _():
        run(first, [small0])
        run(second, [masked, small1])


def dec_forward_kernel(
    big_e, big_d,
    counts_e, counts_d, x, memory, qkv1, wo1, qkv2, wo2, gains,
    xr, q1, k1, v1, mixed1, lse1, after, q2, k2, v2, mixed2, lse2, second,
    ring, bias1, bias2,
):
    length = x.shape[0]
    length_e = memory.shape[0]
    step = big_d
    ends_d, ends_e = bounds(counts_d), bounds(counts_e)
    index_d, start_d = big_plot(counts_d, ends_d, big_d)
    index_e, start_e = big_plot(counts_e, ends_e, big_e)
    gain0 = gains[0:1, :].astype(F32)
    gain1 = gains[1:2, :].astype(F32)
    for r in range(0, length_e, 512):
        m = memory[r : r + 512, :]
        k2[r : r + 512, :] = dot(m, qkv2[1]).astype(BF)
        v2[r : r + 512, :] = dot(m, qkv2[2]).astype(BF)
    fill_rotation(ring, x, length, step + 8)
    project_rows(ring, start_d, length, step, gain0, qkv1.at[0], qkv1.at[1], qkv1.at[2], xr, q1, k1, v1)
    self_bias(bias1, big_d, start_d, ends_d, length)
    pairs = q1.shape[1] // 128
    for rows, parts in self_tiles(big_d, bias1, k1, v1):
        attend(q1, rows, parts, mixed1, lse1, pairs)
    for r in range(0, length, step):
        rows = slice(r, r + step)
        m = xr[rows, :].astype(F32) + dot(mixed1[rows, :], wo1[...])
        after[rows, :] = m
        n = (m * inverse_rms(m) * gain1).astype(BF)
        q2[rows, :] = (dot(n, qkv2[0]).astype(BF) * SCALE).astype(BF)
    cross_setup(ends_d, start_d, big_d, length, index_e, start_e, ends_e, big_e, length_e, bias2)
    seg_col = segments(iota((length - big_d, 1), 0) + big_d, start_d, ends_d, length)
    col = lambda: jnp.where(seg_col == index_e, 0.0, NEG)

    def run(rows, parts):
        attend(q2, rows, parts, mixed2, lse2, pairs)

    cross_run(index_d == index_e, big_d, length, big_e, length_e, col, bias2, k2, v2, run)
    for r in range(0, length, step):
        rows = slice(r, r + step)
        second[rows, :] = after[rows, :] + dot(mixed2[rows, :], wo2[...])


def ffn_back_rows(x, gain, gu, wd, r, n_buf, rb_buf, h_buf, dg_buf, du_buf, rows):
    n = (x * inverse_rms(x) * gain).astype(BF)
    g, u = dot(n, gu[0]), dot(n, gu[1])
    act, t = gelu_parts(g)
    h = (act * u).astype(BF)
    rb = r.astype(BF)
    gh = dot(rb, wd[...], NT)
    slope = 0.5 * (1.0 + t) + (0.5 * GELU_C) * g * (1.0 - t * t) * (1.0 + (3.0 * GELU_A) * g * g)
    dg = (gh * u * slope).astype(BF)
    du = (gh * act).astype(BF)
    n_buf[rows, :] = n
    rb_buf[rows, :] = rb
    h_buf[rows, :] = h
    dg_buf[rows, :] = dg
    du_buf[rows, :] = du
    return h, dot(dg, gu[0], NT) + dot(du, gu[1], NT)


def own_lanes(c, size):
    return pl.ds(pl.multiple_of(c * size, 128), size)


def put_blocks(out, at, value):
    rows, columns = value.shape
    for j in range(0, columns, LANES):
        out[at : at + rows, :] = value[:, j : j + LANES]
        at += rows
    return at


def ffn_weight_grads(core, n_buf, rb_buf, h_buf, dg_buf, du_buf, send, keep):
    half_n, half_h = n_buf.shape[1] // 2, h_buf.shape[1] // 2
    for out, c in ((send, 1 - core), (keep, core)):
        n = n_buf[:, own_lanes(c, half_n)]
        at = put_blocks(out, 0, dot(n, dg_buf[...], TN))
        at = put_blocks(out, at, dot(n, du_buf[...], TN))
        at = put_blocks(out, at, dot(h_buf[:, own_lanes(c, half_h)], rb_buf[...], TN))
        yield out, at, c


def out_proj_grads(places, mixed, rb):
    half = rb.shape[1] // 2
    for out, at, c in places:
        put_blocks(out, at, dot(mixed[...], rb[:, own_lanes(c, half)], TN))


def qkv_grads(core, n_buf, source, dq, dk, dv, send, keep):
    half = n_buf.shape[1] // 2
    for out, c in ((send, 1 - core), (keep, core)):
        lanes = own_lanes(c, half)
        at = put_blocks(out, 0, dot(n_buf[:, lanes], dq[...], TN))
        at = put_blocks(out, at, dot(source[:, lanes], dk[...], TN))
        at = put_blocks(out, at, dot(source[:, lanes], dv[...], TN))
        yield out, at, c


def final_kernel(coords, own, other, *outs):
    for part, c in ((own, coords[0]), (other, 1 - coords[0])):
        at = 0
        for out in outs:
            if len(out.shape) == 2 and out.shape[0] < out.shape[1]:
                rows, half = out.shape[0], out.shape[1] // 2
                for j in range(0, half, LANES):
                    out[:, pl.ds(pl.multiple_of(c * half + j, LANES), LANES)] = part[at : at + rows, :]
                    at += rows
                continue
            for piece in [out.at[i] for i in range(out.shape[0])] if len(out.shape) == 3 else [out]:
                half = piece.shape[0] // 2
                for j in range(0, piece.shape[1], LANES):
                    piece[pl.ds(pl.multiple_of(c * half, 8), half), j : j + LANES] = part[at : at + half, :]
                    at += half


def places_of(h):
    for dp in range(16):
        for y in range(2):
            core, x = dp % 2, (dp // 2) % 2
            first, second = (x, y) if core == 0 else (y, x)
            yield core, first * (h // 2) + second * (h // 4) + (dp // 4) * (h // 16)


def spread_kernel(every, *outs):
    h = every.shape[0] // 2
    share = h // 16
    source = {place: i * share for i, place in enumerate(places_of(h))}

    def copy(out, to, lanes, core, at, rows):
        while rows > 0:
            base = at // share * share
            count = min(rows, base + share - at)
            begin = source[core, base] + at - base
            out[to : to + count, lanes] = every[begin : begin + count, :]
            to, at, rows = to + count, at + count, rows - count

    for core in range(2):
        at = 0
        for out in outs:
            if len(out.shape) == 2 and out.shape[0] < out.shape[1]:
                rows, half = out.shape[0], out.shape[1] // 2
                for j in range(0, half, LANES):
                    copy(out, 0, slice(core * half + j, core * half + j + LANES), core, at, rows)
                    at += rows
                continue
            for piece in [out.at[i] for i in range(out.shape[0])] if len(out.shape) == 3 else [out]:
                half = piece.shape[0] // 2
                for j in range(0, piece.shape[1], LANES):
                    copy(piece, core * half, slice(j, j + LANES), core, at, half)
                    at += half


def row_mask(start, ends, length, r, step):
    slot = wrap(iota((step, 1), 0) + r + start, length)
    return slot < ends[-1]


def dec_ffn_kernel(
    big_d, coords, counts_d, second, cot, gu, wd, gain, wo2, mixed2,
    out, grad_second, go2, send, keep, d_gain,
    ring, n_buf, rb_buf, h_buf, dg_buf, du_buf,
):
    length = second.shape[0]
    step = big_d
    ends = bounds(counts_d)
    _, start = big_plot(counts_d, ends, big_d)
    gain_row = gain[0:1, :].astype(F32)
    fill_rotation(ring, cot, length, step + 8)
    for r in range(0, length, step):
        rows = slice(r, r + step)
        c = rotated_rows(ring, wrap(r + start, length), step)
        grad_second[rows, :] = jnp.where(row_mask(start, ends, length, r, step), c, 0.0)
    total = None
    for r in range(0, length, step):
        rows = slice(r, r + step)
        x = second[rows, :]
        c = grad_second[rows, :]
        h, gn = ffn_back_rows(x, gain_row, gu, wd, c, n_buf, rb_buf, h_buf, dg_buf, du_buf, rows)
        ring[rows, :] = x + dot(h, wd[...])
        gx, gg = norm_back(x, gain_row, gn)
        grad_second[rows, :] = c + gx
        total = gg if total is None else total + gg
    d_gain[...] = total
    places = list(ffn_weight_grads(coords[0], n_buf, rb_buf, h_buf, dg_buf, du_buf, send, keep))
    for r in range(0, length, step):
        rows = slice(r, r + step)
        rb_buf[rows, :] = grad_second[rows, :].astype(BF)
        go2[rows, :] = dot(rb_buf[rows, :], wo2[...], NT).astype(BF)
    out_proj_grads(places, mixed2, rb_buf)
    put_back(ring, start, length, step + 8, step, out)


def enc_ffn_kernel(
    big_e, coords, counts_e, mid, cot, grad_memory, gu, wd, gains, wo, mixed,
    grad_mid, go, send, keep, d_gain,
    ring, n_buf, rb_buf, h_buf, dg_buf, du_buf,
):
    length = mid.shape[0]
    step = length - big_e
    ends = bounds(counts_e)
    _, start = big_plot(counts_e, ends, big_e)
    gain_row = gains[1:2, :].astype(F32)
    fill_rotation(ring, cot, length, step + 8)
    total = None
    for r in range(0, length, step):
        rows = slice(r, r + step)
        c = rotated_rows(ring, wrap(r + start, length), step)
        c = jnp.where(row_mask(start, ends, length, r, step), c, 0.0) + grad_memory[rows, :]
        x = mid[rows, :]
        _, gn = ffn_back_rows(x, gain_row, gu, wd, c, n_buf, rb_buf, h_buf, dg_buf, du_buf, rows)
        gx, gg = norm_back(x, gain_row, gn)
        grad_mid[rows, :] = c + gx
        total = gg if total is None else total + gg
    d_gain[...] = total
    places = list(ffn_weight_grads(coords[0], n_buf, rb_buf, h_buf, dg_buf, du_buf, send, keep))
    for r in range(0, length, step):
        rows = slice(r, r + step)
        rb_buf[rows, :] = grad_mid[rows, :].astype(BF)
        go[rows, :] = dot(rb_buf[rows, :], wo[...], NT).astype(BF)
    out_proj_grads(places, mixed, rb_buf)


def cross_pair_kernel(
    big_e, big_d, counts_e, counts_d, go, q, k, v, mixed, lse, dq, dk, dv, got, qt, dkt, dvt, bias
):
    length, length_e = q.shape[0], k.shape[0]
    ends_d, ends_e = bounds(counts_d), bounds(counts_e)
    index_d, start_d = big_plot(counts_d, ends_d, big_d)
    index_e, start_e = big_plot(counts_e, ends_e, big_e)
    transposes(q, go, qt, got, dkt, dvt)
    cross_setup(ends_d, start_d, big_d, length, index_e, start_e, ends_e, big_e, length_e, bias)
    seg_col = segments(iota((length - big_d, 1), 0) + big_d, start_d, ends_d, length)
    col = lambda: jnp.where(seg_col == index_e, 0.0, NEG)

    def run(rows, parts):
        attend_back(q, qt, go, got, mixed, lse, rows, parts, dq, dkt, dvt, q.shape[1] // 128)

    cross_run(index_d == index_e, big_d, length, big_e, length_e, col, bias, k, v, run)
    turn_back(dkt, dvt, dk, dv)


def transposes(q, go, qt, got, dkt, dvt):
    for r in range(0, q.shape[0], 512):
        qt[:, r : r + 512] = q[r : r + 512, :].T
        got[:, r : r + 512] = go[r : r + 512, :].T
    dkt[...] = jnp.zeros_like(dkt)
    dvt[...] = jnp.zeros_like(dvt)


def turn_back(dkt, dvt, dk, dv):
    for r in range(0, dk.shape[0], 512):
        dk[r : r + 512, :] = dkt[:, r : r + 512].T.astype(BF)
        dv[r : r + 512, :] = dvt[:, r : r + 512].T.astype(BF)


def joined(blocks):
    return jnp.concatenate([b[...] for b in blocks], axis=1)


def cross_tail_kernel(
    coords, grad_second, after, memory, dq0, dq1, dq2, dk0, dk1, dk2, dv0, dv1, dv2, qkv, gains, wo1, mixed1,
    grad_first, grad_memory, go1, send, keep, d_gain, dq, dk, dv, n_buf, rb,
):
    step = 512
    gain_row = gains[1:2, :].astype(F32)
    for i, (a, b, c) in enumerate(((dq0, dk0, dv0), (dq1, dk1, dv1), (dq2, dk2, dv2))):
        sl = slice(i * LANES, (i + 1) * LANES)
        dq[:, sl] = a[...]
        dk[:, sl] = b[...]
        dv[:, sl] = c[...]
    for r in range(0, memory.shape[0], step):
        rows = slice(r, r + step)
        grad_memory[rows, :] = dot(dk[rows, :], qkv[1], NT) + dot(dv[rows, :], qkv[2], NT)
    total = None
    for r in range(0, after.shape[0], step):
        rows = slice(r, r + step)
        x = after[rows, :]
        n_buf[rows, :] = (x * inverse_rms(x) * gain_row).astype(BF)
        gx, gg = norm_back(x, gain_row, dot(dq[rows, :], qkv[0], NT))
        g = grad_second[rows, :] + gx
        grad_first[rows, :] = g
        rb[rows, :] = g.astype(BF)
        go1[rows, :] = dot(rb[rows, :], wo1[...], NT).astype(BF)
        total = gg if total is None else total + gg
    d_gain[...] = total
    out_proj_grads(qkv_grads(coords[0], n_buf, memory, dq, dk, dv, send, keep), mixed1, rb)


def self_tail(core, step, grad, xr, qkv, gain_row, start, dq, dk, dv, n_buf, ring, send, keep, out):
    total = None
    length = xr.shape[0]
    for r in range(0, length, step):
        rows = slice(r, r + step)
        x = xr[rows, :].astype(F32)
        n_buf[rows, :] = (x * inverse_rms(x) * gain_row).astype(BF)
        gn = dot(dq[rows, :], qkv[0], NT) + dot(dk[rows, :], qkv[1], NT) + dot(dv[rows, :], qkv[2], NT)
        gx, gg = norm_back(x, gain_row, gn)
        ring[rows, :] = grad[rows, :] + gx
        total = gg if total is None else total + gg
    for _ in qkv_grads(core, n_buf, n_buf, dq, dk, dv, send, keep):
        pass
    put_back(ring, start, length, step + 8, step, out)
    return total


def dec_self_back_kernel(
    big_d,
    coords, counts_d, go, grad_first, xr, q, k, v, mixed, lse, qkv, gains,
    out, send, keep, d_gain,
    ring, got, qt, dq, dkt, dvt, dk, dv, n_buf, bias,
):
    length = xr.shape[0]
    ends = bounds(counts_d)
    _, start = big_plot(counts_d, ends, big_d)
    transposes(q, go, qt, got, dkt, dvt)
    self_bias(bias, big_d, start, ends, length)
    for rows, parts in self_tiles(big_d, bias, k, v):
        attend_back(q, qt, go, got, mixed, lse, rows, parts, dq, dkt, dvt, q.shape[1] // 128)
    turn_back(dkt, dvt, dk, dv)
    d_gain[...] = self_tail(
        coords[0], big_d, grad_first, xr, qkv, gains[0:1, :].astype(F32), start,
        dq, dk, dv, n_buf, ring, send, keep, out,
    )


def enc_pair_kernel(big_e, counts_e, go, q, k, v, mixed, lse, dq, dk, dv, got, qt, dkt, dvt, bias):
    length = q.shape[0]
    rest = length - big_e
    ends = bounds(counts_e)
    _, start = big_plot(counts_e, ends, big_e)
    transposes(q, go, qt, got, dkt, dvt)
    sq = segments(iota((rest, rest), 0) + big_e, start, ends, length)
    sk = segments(iota((rest, rest), 1) + big_e, start, ends, length)
    bias[...] = jnp.where(sq == sk, 0.0, NEG)
    pairs = q.shape[1] // 128
    for r in range(0, big_e, rest):
        attend_back(q, qt, go, got, mixed, lse, (r, r + rest), [(k, v, 0, big_e, None)], dq, dkt, dvt, pairs)
    parts = [(k, v, big_e, length, lambda: bias[...])]
    attend_back(q, qt, go, got, mixed, lse, (big_e, length), parts, dq, dkt, dvt, pairs)
    turn_back(dkt, dvt, dk, dv)


def enc_tail_kernel(
    big_e,
    coords, counts_e, grad_mid, xr, dq0, dq1, dq2, dk0, dk1, dk2, dv0, dv1, dv2, qkv, gains,
    gain_e2, gain_d1, gain_d2, gain_d3,
    out, send, keep, ring, dq, dk, dv, n_buf,
):
    rest = xr.shape[0] - big_e
    _, start = big_plot(counts_e, bounds(counts_e), big_e)
    for i, (a, b, c) in enumerate(((dq0, dk0, dv0), (dq1, dk1, dv1), (dq2, dk2, dv2))):
        sl = slice(i * LANES, (i + 1) * LANES)
        dq[:, sl] = a[...]
        dk[:, sl] = b[...]
        dv[:, sl] = c[...]
    gain_e1 = self_tail(
        coords[0], rest, grad_mid, xr, qkv, gains[0:1, :].astype(F32), start, dq, dk, dv, n_buf, ring, send, keep, out
    )
    rows = []
    for gain in (gain_e1, gain_e2[...], gain_d1[...], gain_d2[...], gain_d3[...]):
        rows += [gain[:, j : j + LANES] for j in range(0, gain.shape[1], LANES)]
    at = keep.shape[0] - EXTRA
    for ref in (send, keep):
        ref[at:, :] = jnp.zeros((EXTRA, LANES), F32)
        for i, row in enumerate(rows):
            ref[at + i : at + i + 1, :] = row


LANES = 128


def pairs_of(size, bit):
    return [(i, i ^ bit) for i in range(size)]


def turns_of(size, unit, count, by):
    out = []
    for i in range(size):
        place = (i // unit) % count
        out.append((i, i + ((place + by) % count - place) * unit))
    return out


def step_kernel(n_in, jobs, coords, *refs):
    where = tuple(coords[i] for i in range(4))
    ins, outs = refs[:n_in], refs[n_in:]
    for out, at, rows, terms in jobs:
        chunk = next(c for c in (512, 384, 256, 192, 128, 96, 64, 48, 32, 24, 16, 8) if rows % c == 0)
        to = at(where) if callable(at) else at
        froms = [(i, off(where) if callable(off) else off) for i, off in terms]

        def one(j, carry, out=out, to=to, froms=froms, chunk=chunk):
            def place(base):
                return pl.ds(pl.multiple_of(base + j * chunk, 8), chunk)

            total = ins[froms[0][0]][place(froms[0][1]), :]
            for i, off in froms[1:]:
                total = total + ins[i][place(off), :]
            outs[out][place(to), :] = total
            return carry

        lax.fori_loop(0, rows // chunk, one, 0)


class Chain:
    def __init__(self):
        self.last = None

    def __call__(self, kernel, name, scalars, arrays, outs, scratch, flops, limit, blocks=None):
        vmem = pl.BlockSpec(memory_space=pltpu.VMEM)
        smem = pl.BlockSpec(memory_space=pltpu.SMEM)
        before = [] if self.last is None else [self.last]
        size = sum(a.size * a.dtype.itemsize for a in (*arrays, *outs))
        count = len(scalars) + len(arrays)

        def body(*refs):
            kernel(*refs[:count], *refs[count + len(before) :])

        specs = [vmem] * len(arrays)
        for i, spec in (blocks or {}).items():
            specs[i] = spec
        got = pl.pallas_call(
            body,
            out_shape=tuple(outs),
            in_specs=[smem] * len(scalars) + specs + [pl.BlockSpec(memory_space=pl.ANY)] * len(before),
            out_specs=tuple([vmem] * len(outs)),
            scratch_shapes=[pltpu.VMEM(s, d) for s, d in scratch],
            compiler_params=pltpu.CompilerParams(vmem_limit_bytes=limit),
            cost_estimate=pl.CostEstimate(flops=0 if name in SHORT else flops * HINT, bytes_accessed=0, transcendentals=0),
            name=name,
            **({"grid": (1,)} if blocks else {}),
        )(*scalars, *arrays, *before)
        self.last = min(got, key=lambda o: o.size * o.dtype.itemsize)
        return got


def run_step(chain, name, coords, arrays, out_rows, jobs):
    moved = 4 * LANES * (sum(a.shape[0] for a in arrays) + sum(out_rows))
    outs = [jax.ShapeDtypeStruct((r, LANES), F32) for r in out_rows]
    kernel = functools.partial(step_kernel, len(arrays), jobs)
    return chain(kernel, name, [coords], arrays, outs, [], 0, moved + (2 << 20))


def swap(v, first):
    dp, batch = lax.axis_size("dp"), lax.axis_size("batch")
    out = []
    for i in range(dp):
        for j in range(batch):
            along_x = (i % 2 == 0) == first
            out.append((i * batch + j, (i ^ 2) * batch + j if along_x else i * batch + (j ^ 1)))
    return lax.ppermute(v, AXES, out)


def core_swap(v):
    return lax.ppermute(v, "dp", pairs_of(lax.axis_size("dp"), 1))


def z_send(v, by):
    return lax.ppermute(v, "dp", turns_of(lax.axis_size("dp"), 4, 4, by))


def over_rest(values):
    size = lax.axis_size("dp")
    if size == 16:
        return values
    groups = [list(range(i, size, 16)) for i in range(16)]
    return [lax.psum(v, "dp", axis_index_groups=groups) for v in values]


def reduce_gather(chain, coords, send, keep, extra, tag, whole=False):
    h = keep.shape[0] - extra
    got = core_swap(send)
    rows, now = h, [keep, got]
    for level in (1, 2):
        yield
        rows //= 2
        mine = lambda w, level=level, rows=rows: w[level] * rows
        theirs = lambda w, level=level, rows=rows: (1 - w[level]) * rows
        jobs = [(0, 0, rows, [(0, theirs), (1, theirs)]), (1, 0, rows, [(0, mine), (1, mine)])]
        if extra:
            jobs += [(o, rows, extra, [(0, 2 * rows), (1, 2 * rows)]) for o in (0, 1)]
        out, kept = run_step(chain, f"sum{level}_{tag}", coords, now, [rows + extra] * 2, jobs)
        now = [kept, swap(out, level == 1)]
    yield
    e, p = rows, rows // 4
    jobs = []
    for d in range(4):
        off = lambda w, d=d: ((w[3] + d) % 4) * p
        jobs.append((d, 0, p, [(0, off), (1, off)]))
        if extra:
            jobs.append((d, p, extra, [(0, e), (1, e)]))
    parts = run_step(chain, f"sum3_{tag}", coords, now, [p + extra] * 4, jobs)
    parts = [parts[0]] + [z_send(parts[d], d) for d in (1, 2, 3)]
    yield
    jobs = [(0, 0, p, [(i, 0) for i in range(4)])]
    if extra:
        jobs.append((1, 0, extra, [(i, p) for i in range(4)]))
    done = over_rest(run_step(chain, f"sum4_{tag}", coords, parts, [p] + [extra] * (extra > 0), jobs))
    own, total = done[0], (done[1] if extra else None)
    if whole:
        every = lax.all_gather(own, AXES, axis=0, tiled=True)
        yield
        return every, None, total
    parts = [own] + [z_send(own, d) for d in (1, 2, 3)]
    yield
    jobs = [(0, lambda w, d=d: ((w[3] + 4 - d) % 4) * p, p, [(d, 0)]) for d in range(4)]
    (part,) = run_step(chain, f"put5_{tag}", coords, parts, [e], jobs)
    for level in (2, 1):
        other = swap(part, level == 1)
        yield
        mine = lambda w, level=level, rows=rows: w[level] * rows
        theirs = lambda w, level=level, rows=rows: (1 - w[level]) * rows
        jobs = [(0, mine, rows, [(0, 0)]), (0, theirs, rows, [(1, 0)])]
        rows *= 2
        (part,) = run_step(chain, f"put{8 - level}_{tag}", coords, [part, other], [rows], jobs)
    other = core_swap(part)
    yield
    return part, other, total


def coords_of():
    dp, y = lax.axis_index("dp"), lax.axis_index("batch")
    core, x = dp % 2, (dp // 2) % 2
    first, second = jnp.where(core == 0, x, y), jnp.where(core == 0, y, x)
    return jnp.stack([core, first, second, (dp // 4) % 4]).astype(jnp.int32)


def like(shape, dtype):
    return jax.ShapeDtypeStruct(shape, dtype)


class Group:
    def __init__(self, chain, coords, pair, extra, outs, tag, whole=False):
        self.chain, self.coords, self.outs, self.tag = chain, coords, outs, tag
        self.whole = whole and lax.axis_size("dp") == 16
        self.work = reduce_gather(chain, coords, *pair, extra, tag, self.whole)
        self.result = None
        next(self.work)

    def step(self):
        try:
            next(self.work)
        except StopIteration as end:
            own, other, self.total = end.value
            size = 8 * sum(o.size for o in self.outs)
            if self.whole:
                self.result = self.chain(
                    spread_kernel, f"final_{self.tag}", [], [own], self.outs, [], 0, size + (4 << 20)
                )
                return
            self.result = self.chain(
                final_kernel, f"final_{self.tag}", [self.coords], [own, other], self.outs, [], 0, size + (4 << 20)
            )


def shards(
    enc_input, dec_input, patch_counts, table_lengths,
    enc_qkv, enc_wo, enc_gu, enc_wd, enc_gains,
    self_qkv, self_wo, cross_qkv, cross_wo, dec_gu, dec_wd, dec_gains, dec_gain, enc_cot, dec_cot,
):
    chain = Chain()
    coords = coords_of()
    le, width = enc_input.shape[1:]
    ld = dec_input.shape[1]
    inner = enc_wo.shape[0]
    ff = enc_wd.shape[0]
    big_e, big_d = le - le // 4, ld // 2
    rest_e = le - big_e
    enc_row, dec_row, counts, lengths = enc_input[0], dec_input[0], patch_counts, table_lengths
    limit = 58 << 20
    third = lambda i: pl.BlockSpec((le, LANES), lambda _: (0, i))
    third_d = lambda i: pl.BlockSpec((ld, LANES), lambda _: (0, i))
    groups = {}

    out_e, memory, xr_e, q_e, k_e, v_e, mixed_e, lse_e, mid = chain(
        functools.partial(enc_forward_kernel, big_e), "enc_forward",
        [counts], [enc_row, enc_qkv, enc_wo, enc_gu, enc_wd, enc_gains],
        [like((le, width), BF)] * 3 + [like((le, inner), BF)] * 4 + [like((le, inner), F32), like((le, width), F32)],
        [((le + rest_e + 8, width), F32), ((rest_e, rest_e), F32)], 11_000_000_000, limit,
    )
    xr_d, q1, k1, v1, mixed1, lse1, after, q2, k2, v2, mixed2, lse2, second = chain(
        functools.partial(dec_forward_kernel, big_e, big_d), "dec_forward",
        [counts, lengths], [dec_row, memory, self_qkv, self_wo, cross_qkv, cross_wo, dec_gains],
        [like((ld, width), BF)] + [like((ld, inner), BF)] * 4 + [like((ld, inner), F32), like((ld, width), F32)]
        + [like((ld, inner), BF), like((le, inner), BF), like((le, inner), BF), like((ld, inner), BF)]
        + [like((ld, inner), F32), like((ld, width), F32)],
        [((ld + big_d + 8, width), F32), ((2, big_d, big_d), F32), ((2, ld - big_d, rest_e), F32)],
        8_000_000_000, limit,
    )

    def ffn_scratch(length, extra):
        return [((length + extra + 8, width), F32), ((length, width), BF), ((length, width), BF)] + [((length, ff), BF)] * 3

    def pair_scratch(lq, lk):
        return [((LANES, lq), BF), ((LANES, lq), BF), ((LANES, lk), F32), ((LANES, lk), F32)]

    def grads(*sizes, extra=0):
        return [like((sum(sizes) // 2 // LANES + extra, LANES), F32)] * 2

    ffn_size, qkv_size, wo_size = 3 * width * ff, 3 * width * inner, inner * width
    ffn_outs = [like((2, width, ff), F32), like((ff, width), F32), like((inner, width), F32)]
    qkv_outs = [like((3, width, inner), F32)]
    wo_outs = [like((inner, width), F32)]
    gain_out = [like((1, width), F32)]

    out_d, grad_second, go2, *sums, d_gain3 = chain(
        functools.partial(dec_ffn_kernel, big_d), "dec_ffn",
        [coords, lengths], [second, dec_cot[0], dec_gu, dec_wd, dec_gain.reshape(1, width), cross_wo, mixed2],
        [like((ld, width), BF), like((ld, width), F32), like((ld, inner), BF)] + grads(ffn_size, wo_size) + gain_out,
        ffn_scratch(ld, big_d), 10_000_000_000, limit,
    )
    groups[1] = Group(chain, coords, sums, 0, ffn_outs, "dec_ffn", True)

    def advance(*numbers):
        for number in numbers:
            if groups[number].result is None:
                groups[number].step()

    blocks = []
    for i in range(3):
        blocks.append(
            chain(
                functools.partial(cross_pair_kernel, big_e, big_d), f"cross_pair{i}",
                [counts, lengths], [go2, q2, k2, v2, mixed2, lse2],
                [like((ld, LANES), BF), like((le, LANES), BF), like((le, LANES), BF)],
                pair_scratch(ld, le) + [((2, ld - big_d, rest_e), F32)], 4_000_000_000, PAIR_LIMIT,
                {0: third_d(i), 1: third_d(i), 2: third(i), 3: third(i), 4: third_d(i), 5: third_d(i)},
            )
        )
        advance(*PLAN["cross", i])
    dq, dk, dv = zip(*blocks)
    grad_first, grad_memory, go1, *sums, d_gain2 = chain(
        cross_tail_kernel, "cross_tail",
        [coords], [grad_second, after, memory, *dq, *dk, *dv, cross_qkv, dec_gains, self_wo, mixed1],
        [like((ld, width), F32), like((le, width), F32), like((ld, inner), BF)] + grads(qkv_size, wo_size) + gain_out,
        [((ld, inner), BF), ((le, inner), BF), ((le, inner), BF), ((ld, width), BF), ((ld, width), BF)],
        4_000_000_000, limit,
    )
    groups[2] = Group(chain, coords, sums, 0, qkv_outs + wo_outs, "cross")
    advance(*PLAN["cross_tail"])
    grad_mid, go_e, *sums, d_enc_gain2 = chain(
        functools.partial(enc_ffn_kernel, big_e), "enc_ffn",
        [coords, counts], [mid, enc_cot[0], grad_memory, enc_gu, enc_wd, enc_gains, enc_wo, mixed_e],
        [like((le, width), F32), like((le, inner), BF)] + grads(ffn_size, wo_size) + gain_out,
        ffn_scratch(le, rest_e), 14_000_000_000, limit,
    )
    groups[3] = Group(chain, coords, sums, 0, ffn_outs, "enc_ffn")
    advance(*PLAN["enc_ffn"])
    grad_dec, *sums, d_gain1 = chain(
        functools.partial(dec_self_back_kernel, big_d), "dec_self_back",
        [coords, lengths], [go1, grad_first, xr_d, q1, k1, v1, mixed1, lse1, self_qkv, dec_gains],
        [like((ld, width), F32)] + grads(qkv_size) + gain_out,
        [
            ((ld + big_d + 8, width), F32), ((inner, ld), BF), ((inner, ld), BF), ((ld, inner), BF),
            ((inner, ld), F32), ((inner, ld), F32), ((ld, inner), BF), ((ld, inner), BF), ((ld, width), BF),
            ((2, big_d, big_d), F32),
        ],
        6_000_000_000, limit,
    )
    groups[4] = Group(chain, coords, sums, 0, qkv_outs, "dec_self")
    advance(*PLAN["dec_self"])
    blocks = []
    for i in range(3):
        blocks.append(
            chain(
                functools.partial(enc_pair_kernel, big_e), f"enc_pair{i}",
                [counts], [go_e, q_e, k_e, v_e, mixed_e, lse_e],
                [like((le, LANES), BF)] * 3,
                pair_scratch(le, le) + [((rest_e, rest_e), F32)], 5_000_000_000, PAIR_LIMIT,
                {j: third(i) for j in range(6)},
            )
        )
        advance(*PLAN["enc", i])
    dq, dk, dv = zip(*blocks)
    grad_enc, *sums = chain(
        functools.partial(enc_tail_kernel, big_e), "enc_tail",
        [coords, counts],
        [grad_mid, xr_e, *dq, *dk, *dv, enc_qkv, enc_gains, d_enc_gain2, d_gain1, d_gain2, d_gain3],
        [like((le, width), F32)] + grads(qkv_size, extra=EXTRA),
        [((le + rest_e + 8, width), F32)] + [((le, inner), BF)] * 3 + [((le, width), BF)],
        6_000_000_000, limit,
    )
    groups[5] = Group(chain, coords, sums, EXTRA, qkv_outs, "enc_self")
    advance(*PLAN["enc_tail"])
    while any(group.result is None for group in groups.values()):
        advance(*TAIL)

    d_dec_gu, d_dec_wd, d_cross_wo = groups[1].result
    d_cross_qkv, d_self_wo = groups[2].result
    d_enc_gu, d_enc_wd, d_enc_wo = groups[3].result
    (d_self_qkv,) = groups[4].result
    (d_enc_qkv,) = groups[5].result
    gains = groups[5].total[: 5 * width // LANES].reshape(5, width)
    return (
        out_e[None], out_d[None], grad_enc[None], grad_dec[None],
        d_enc_qkv, d_enc_wo, d_enc_gu, d_enc_wd, gains[0:2],
        d_self_qkv, d_self_wo, d_cross_qkv, d_cross_wo, d_dec_gu, d_dec_wd, gains[2:4], gains[4],
    )


HINT = 20
SHORT = ('cross_pair2', 'cross_tail')
PAIR_LIMIT = 40 << 20
PLAN = {
    ("cross", 0): (1,),
    ("cross", 1): (),
    ("cross", 2): (),
    "cross_tail": (1,),
    "enc_ffn": (1, 2),
    "dec_self": (1, 2, 3),
    ("enc", 0): (2, 4),
    ("enc", 1): (3, 2),
    ("enc", 2): (4, 3, 2),
    "enc_tail": (),
}
TAIL = (4, 3, 5, 2, 4, 5, 3, 2, 5, 4, 3, 5, 2, 4, 3, 5, 4, 5, 3, 1, 4, 5, 3, 5)


def solution(mesh):
    rows3 = P(AXES, None, None)
    rows2 = P(AXES, None)
    return jax.shard_map(
        shards,
        mesh=mesh,
        in_specs=(rows3, rows3, rows2, rows2) + (P(),) * 13 + (rows3, rows3),
        out_specs=(rows3,) * 4 + (P(),) * 13,
        check_vma=False,
    )
```

```python
import functools

import jax
import jax.numpy as jnp
from jax import lax
from jax.experimental import pallas as pl
from jax.experimental.pallas import tpu as pltpu
from jax.sharding import PartitionSpec as P

BF = jnp.bfloat16
F32 = jnp.float32
EPS = 1e-06
NEG = -1e30
SCALE = 0.125
PLAIN = (((1,), (0,)), ((), ()))
NT = (((1,), (1,)), ((), ()))
TN = (((0,), (0,)), ((), ()))
AXES = ("dp", "batch")
GELU_C = 0.7978845608028654
GELU_A = 0.044715
EXTRA = 24


def dot(a, b, dims=PLAIN):
    return lax.dot_general(a, b, dims, preferred_element_type=F32)


def bounds(counts):
    ends, total = [], 0
    for p in range(counts.shape[1]):
        total = total + counts[0, p]
        ends.append(total)
    return ends


def big_plot(counts, ends, size):
    index, start = jnp.int32(0), jnp.int32(0)
    for p in range(1, counts.shape[1]):
        hit = counts[0, p] == size
        index = jnp.where(hit, p, index)
        start = jnp.where(hit, ends[p - 1], start)
    return index, start


def segments(rotated, start, ends, length):
    slot = rotated + start
    slot = jnp.where(slot >= length, slot - length, slot)
    seg = jnp.zeros(rotated.shape, jnp.int32)
    for end in ends:
        seg = seg + (slot >= end).astype(jnp.int32)
    return seg


def iota(shape, dim):
    return lax.broadcasted_iota(jnp.int32, shape, dim)


def wrap(offset, length):
    return jnp.where(offset >= length, offset - length, offset)


def inverse_rms(x):
    return lax.rsqrt(jnp.mean(x * x, axis=1, keepdims=True) + EPS)


def norm_back(x, gain, grad):
    s = inverse_rms(x)
    xs = x * s
    gg = grad * gain
    inner = jnp.mean(gg * xs, axis=1, keepdims=True)
    return s * (gg - xs * inner), jnp.sum(grad * xs, axis=0, keepdims=True)


def fill_rotation(ring, source, length, extra, step=128):
    for r in range(0, length, step):
        ring[r : r + step, :] = source[r : r + step, :].astype(F32)
    ring[length : length + extra, :] = ring[0:extra, :]


def rotated_rows(ring, offset, count):
    base = pl.multiple_of((offset // 8) * 8, 8)
    sub = offset - base
    block = ring[pl.ds(base, count + 8), :]
    shape = (count // 8, 8, block.shape[1])
    turn = lax.rem(8 - sub, 8)
    first = pltpu.roll(block[0:count].reshape(shape), turn, 1)
    second = pltpu.roll(block[8 : count + 8].reshape(shape), turn, 1)
    return jnp.where(iota(shape, 1) < 8 - sub, first, second).reshape(count, shape[2])


def lanes_low(rows):
    return iota((rows, 128), 1) < 64


def head_of(x, low, h):
    zero = jnp.zeros_like(x)
    return jnp.where(low, x, zero) if h == 0 else jnp.where(low, zero, x)


def with_ones(v, low, h):
    one = jnp.ones_like(v)
    return jnp.where(low, v, one) if h == 0 else jnp.where(low, one, v)


def scores_of(qh, parts, sl):
    out = []
    for k, _, lo, hi, bias in parts:
        s = dot(qh, k[lo:hi, sl], NT)
        if bias is not None:
            s = s + bias()
        out.append(s)
    return out


def attend(q, rows, parts, mixed, lse, pairs):
    r0, r1 = rows
    low = lanes_low(r1 - r0)
    for pair in range(pairs):
        sl = slice(pair * 128, pair * 128 + 128)
        qp = q[r0:r1, sl]
        accs, tops = [], []
        for h in range(2):
            all_s = scores_of(head_of(qp, low, h), parts, sl)
            top = jnp.max(all_s[0], axis=1, keepdims=True)
            for s in all_s[1:]:
                top = jnp.maximum(top, jnp.max(s, axis=1, keepdims=True))
            acc = None
            for s, (_, v, lo, hi, _) in zip(all_s, parts):
                p = jnp.exp(s - top).astype(BF)
                term = dot(p, with_ones(v[lo:hi, sl], lanes_low(hi - lo), h))
                acc = term if acc is None else acc + term
            accs.append(acc)
            tops.append(top)
        total = pltpu.roll(jnp.where(low, accs[1], accs[0]), 64, 1)
        mixed[r0:r1, sl] = (jnp.where(low, accs[0], accs[1]) / total).astype(BF)
        lse[r0:r1, sl] = jnp.where(low, tops[0], tops[1]) + jnp.log(total)


def attend_back(q, qt, go, got, mixed, lse, rows, parts, dq, dkt, dvt, pairs):
    r0, r1 = rows
    low = lanes_low(r1 - r0)
    for pair in range(pairs):
        sl = slice(pair * 128, pair * 128 + 128)
        qp, gp = q[r0:r1, sl], go[r0:r1, sl]
        inner = gp.astype(F32) * mixed[r0:r1, sl].astype(F32)
        halves = []
        for h in range(2):
            hs = slice(pair * 128 + h * 64, pair * 128 + h * 64 + 64)
            qh, gh = head_of(qp, low, h), head_of(gp, low, h)
            delta = jnp.sum(head_of(inner, low, h), axis=1, keepdims=True)
            log_total = lse[r0:r1, hs.start : hs.start + 1]
            dq_h = None
            for s, (k, v, lo, hi, _) in zip(scores_of(qh, parts, sl), parts):
                p = jnp.exp(s - log_total)
                dp = dot(gh, v[lo:hi, sl], NT)
                ds = (p * (dp - delta)).astype(BF)
                dvt[hs, lo:hi] += dot(got[hs, r0:r1], p.astype(BF))
                dkt[hs, lo:hi] += dot(qt[hs, r0:r1], ds)
                term = dot(ds, k[lo:hi, sl])
                dq_h = term if dq_h is None else dq_h + term
            halves.append(dq_h)
        dq[r0:r1, sl] = (jnp.where(low, halves[0], halves[1]) * SCALE).astype(BF)


def gelu_parts(g):
    t = jnp.tanh(GELU_C * (g + GELU_A * g * g * g))
    return 0.5 * g * (1.0 + t), t


def project_rows(ring, start, length, step, gain, wq, wk, wv, xr, q, k, v):
    for r in range(0, length, step):
        x = rotated_rows(ring, wrap(r + start, length), step)
        xr[r : r + step, :] = x.astype(BF)
        n = (x * inverse_rms(x) * gain).astype(BF)
        q[r : r + step, :] = (dot(n, wq[...]).astype(BF) * SCALE).astype(BF)
        k[r : r + step, :] = dot(n, wk[...]).astype(BF)
        v[r : r + step, :] = dot(n, wv[...]).astype(BF)


def put_back(ring, start, length, extra, step, out):
    ring[length : length + extra, :] = ring[0:extra, :]
    for r in range(0, length, step):
        at = r - start
        at = jnp.where(at < 0, at + length, at)
        out[r : r + step, :] = rotated_rows(ring, at, step).astype(out.dtype)


def enc_forward_kernel(
    big, counts, x, qkv, wo, gu, wd, gains, out, memory, xr, q, k, v, mixed, lse, mid, ring, bias
):
    length = x.shape[0]
    rest = length - big
    step = rest
    ends = bounds(counts)
    _, start = big_plot(counts, ends, big)
    gain0 = gains[0:1, :].astype(F32)
    gain1 = gains[1:2, :].astype(F32)
    ready(x)
    fill_rotation(ring, x, length, step + 8)
    ready(qkv)
    project_rows(ring, start, length, step, gain0, qkv.at[0], qkv.at[1], qkv.at[2], xr, q, k, v)
    store(xr, q, k, v)
    sq = segments(iota((rest, rest), 0) + big, start, ends, length)
    sk = segments(iota((rest, rest), 1) + big, start, ends, length)
    bias[...] = jnp.where(sq == sk, 0.0, NEG)
    pairs = q.shape[1] // 128
    for r in range(0, big, step):
        attend(q, (r, r + step), [(k, v, 0, big, None)], mixed, lse, pairs)
    attend(q, (big, length), [(k, v, big, length, lambda: bias[...])], mixed, lse, pairs)
    store(mixed, lse)
    ready(wo, gu, wd)
    for r in range(0, length, step):
        rows = slice(r, r + step)
        m = xr[rows, :].astype(F32) + dot(mixed[rows, :], wo[...])
        mid[rows, :] = m
        n = (m * inverse_rms(m) * gain1).astype(BF)
        act, _ = gelu_parts(dot(n, gu[0]))
        hidden = (act * dot(n, gu[1])).astype(BF)
        total = m + dot(hidden, wd[...])
        ring[rows, :] = total
        memory[rows, :] = total.astype(BF)
    store(mid, memory)
    put_back(ring, start, length, step + 8, step, out)


def self_bias(bias, big, start, ends, length):
    shape = (big, big)
    row, col = iota(shape, 0), iota(shape, 1)
    bias[0, :, :] = jnp.where(row >= col, 0.0, NEG)
    same = segments(row + big, start, ends, length) == segments(col + big, start, ends, length)
    bias[1, :, :] = jnp.where(jnp.logical_and(row >= col, same), 0.0, NEG)


def self_tiles(big, bias, k, v):
    half = big // 2
    for b in range(2):
        at = b * big
        for t in range(2):
            lo, hi = t * half, (t + 1) * half
            part = (k, v, at, at + hi, lambda b=b, lo=lo, hi=hi: bias[b, lo:hi, 0:hi])
            yield (at + lo, at + hi), [part]


def cross_setup(ends_d, start_d, big_d, length_d, index_e, start_e, ends_e, big_e, length_e, bias):
    shape = (length_d - big_d, length_e - big_e)
    key = segments(iota(shape, 1) + big_e, start_e, ends_e, length_e)
    for b in range(2):
        query = segments(iota(shape, 0) + b * big_d, start_d, ends_d, length_d)
        bias[b, :, :] = jnp.where(query == key, 0.0, NEG)


def cross_run(same, big_d, length_d, big_e, length_e, rest_col, bias, k, v, run):
    first, second = (0, big_d), (big_d, length_d)
    whole = (k, v, 0, big_e, None)
    masked = (k, v, 0, big_e, rest_col)
    small0 = (k, v, big_e, length_e, lambda: bias[0])
    small1 = (k, v, big_e, length_e, lambda: bias[1])

    @pl.when(same)
    def _():
        run(first, [whole])
        run(second, [small1])

    @pl.when(jnp.logical_not(same))
    def _():
        run(first, [small0])
        run(second, [masked, small1])


def dec_forward_kernel(
    big_e, big_d,
    counts_e, counts_d, x, memory, qkv1, wo1, qkv2, wo2, gains,
    xr, q1, k1, v1, mixed1, lse1, after, q2, k2, v2, mixed2, lse2, second,
    ring, bias1, bias2,
):
    length = x.shape[0]
    length_e = memory.shape[0]
    step = big_d
    ends_d, ends_e = bounds(counts_d), bounds(counts_e)
    index_d, start_d = big_plot(counts_d, ends_d, big_d)
    index_e, start_e = big_plot(counts_e, ends_e, big_e)
    gain0 = gains[0:1, :].astype(F32)
    gain1 = gains[1:2, :].astype(F32)
    ready(memory, qkv2)
    for r in range(0, length_e, 512):
        m = memory[r : r + 512, :]
        k2[r : r + 512, :] = dot(m, qkv2[1]).astype(BF)
        v2[r : r + 512, :] = dot(m, qkv2[2]).astype(BF)
    store(k2, v2)
    ready(x, qkv1)
    fill_rotation(ring, x, length, step + 8)
    project_rows(ring, start_d, length, step, gain0, qkv1.at[0], qkv1.at[1], qkv1.at[2], xr, q1, k1, v1)
    store(xr, q1, k1, v1)
    self_bias(bias1, big_d, start_d, ends_d, length)
    pairs = q1.shape[1] // 128
    for rows, parts in self_tiles(big_d, bias1, k1, v1):
        attend(q1, rows, parts, mixed1, lse1, pairs)
    store(mixed1, lse1)
    ready(wo1)
    for r in range(0, length, step):
        rows = slice(r, r + step)
        m = xr[rows, :].astype(F32) + dot(mixed1[rows, :], wo1[...])
        after[rows, :] = m
        n = (m * inverse_rms(m) * gain1).astype(BF)
        q2[rows, :] = (dot(n, qkv2[0]).astype(BF) * SCALE).astype(BF)
    store(after, q2)
    cross_setup(ends_d, start_d, big_d, length, index_e, start_e, ends_e, big_e, length_e, bias2)
    seg_col = segments(iota((length - big_d, 1), 0) + big_d, start_d, ends_d, length)
    col = lambda: jnp.where(seg_col == index_e, 0.0, NEG)

    def run(rows, parts):
        attend(q2, rows, parts, mixed2, lse2, pairs)

    cross_run(index_d == index_e, big_d, length, big_e, length_e, col, bias2, k2, v2, run)
    store(mixed2, lse2)
    ready(wo2)
    for r in range(0, length, step):
        rows = slice(r, r + step)
        second[rows, :] = after[rows, :] + dot(mixed2[rows, :], wo2[...])


def ffn_back_rows(x, gain, gu, wd, r, n_buf, rb_buf, h_buf, dg_buf, du_buf, rows):
    n = (x * inverse_rms(x) * gain).astype(BF)
    g, u = dot(n, gu[0]), dot(n, gu[1])
    act, t = gelu_parts(g)
    h = (act * u).astype(BF)
    rb = r.astype(BF)
    gh = dot(rb, wd[...], NT)
    slope = 0.5 * (1.0 + t) + (0.5 * GELU_C) * g * (1.0 - t * t) * (1.0 + (3.0 * GELU_A) * g * g)
    dg = (gh * u * slope).astype(BF)
    du = (gh * act).astype(BF)
    n_buf[rows, :] = n
    rb_buf[rows, :] = rb
    h_buf[rows, :] = h
    dg_buf[rows, :] = dg
    du_buf[rows, :] = du
    return h, dot(dg, gu[0], NT) + dot(du, gu[1], NT)


def own_lanes(c, size):
    return pl.ds(pl.multiple_of(c * size, 128), size)


def put_blocks(out, at, value):
    rows, columns = value.shape
    for j in range(0, columns, LANES):
        out[at : at + rows, :] = value[:, j : j + LANES]
        at += rows
    return at


def ffn_weight_grads(core, n_buf, rb_buf, h_buf, dg_buf, du_buf, send, keep):
    half_n, half_h = n_buf.shape[1] // 2, h_buf.shape[1] // 2
    for out, c in ((send, 1 - core), (keep, core)):
        n = n_buf[:, own_lanes(c, half_n)]
        at = put_blocks(out, 0, dot(n, dg_buf[...], TN))
        at = put_blocks(out, at, dot(n, du_buf[...], TN))
        at = put_blocks(out, at, dot(h_buf[:, own_lanes(c, half_h)], rb_buf[...], TN))
        yield out, at, c


def out_proj_grads(places, mixed, rb):
    half = rb.shape[1] // 2
    for out, at, c in places:
        put_blocks(out, at, dot(mixed[...], rb[:, own_lanes(c, half)].astype(BF), TN))
        store(out)


def qkv_grads(core, n_buf, source, dq, dk, dv, send, keep):
    half = n_buf.shape[1] // 2
    for out, c in ((send, 1 - core), (keep, core)):
        lanes = own_lanes(c, half)
        at = put_blocks(out, 0, dot(n_buf[:, lanes], dq[...], TN))
        at = put_blocks(out, at, dot(source[:, lanes], dk[...], TN))
        at = put_blocks(out, at, dot(source[:, lanes], dv[...], TN))
        yield out, at, c


def final_kernel(coords, own, other, *outs):
    for part, c in ((own, coords[0]), (other, 1 - coords[0])):
        at = 0
        for out in outs:
            if len(out.shape) == 2 and out.shape[0] < out.shape[1]:
                rows, half = out.shape[0], out.shape[1] // 2
                for j in range(0, half, LANES):
                    out[:, pl.ds(pl.multiple_of(c * half + j, LANES), LANES)] = part[at : at + rows, :]
                    at += rows
                continue
            for piece in [out.at[i] for i in range(out.shape[0])] if len(out.shape) == 3 else [out]:
                half = piece.shape[0] // 2
                for j in range(0, piece.shape[1], LANES):
                    piece[pl.ds(pl.multiple_of(c * half, 8), half), j : j + LANES] = part[at : at + half, :]
                    at += half


def places_of(h):
    for dp in range(16):
        for y in range(2):
            core, x = dp % 2, (dp // 2) % 2
            first, second = (x, y) if core == 0 else (y, x)
            yield core, first * (h // 2) + second * (h // 4) + (dp // 4) * (h // 16)


def spread_kernel(every, *outs):
    h = every.shape[0] // 2
    share = h // 16
    source = {place: i * share for i, place in enumerate(places_of(h))}

    def copy(out, to, lanes, core, at, rows):
        while rows > 0:
            base = at // share * share
            count = min(rows, base + share - at)
            begin = source[core, base] + at - base
            out[to : to + count, lanes] = every[begin : begin + count, :]
            to, at, rows = to + count, at + count, rows - count

    for core in range(2):
        at = 0
        for out in outs:
            if len(out.shape) == 2 and out.shape[0] < out.shape[1]:
                rows, half = out.shape[0], out.shape[1] // 2
                for j in range(0, half, LANES):
                    copy(out, 0, slice(core * half + j, core * half + j + LANES), core, at, rows)
                    at += rows
                continue
            for piece in [out.at[i] for i in range(out.shape[0])] if len(out.shape) == 3 else [out]:
                half = piece.shape[0] // 2
                for j in range(0, piece.shape[1], LANES):
                    copy(piece, core * half, slice(j, j + LANES), core, at, half)
                    at += half


def row_mask(start, ends, length, r, step):
    slot = wrap(iota((step, 1), 0) + r + start, length)
    return slot < ends[-1]


def dec_ffn_kernel(
    big_d, coords, counts_d, second, cot, gu, wd, gain, wo2, mixed2,
    out, grad_second, go2, send, keep, d_gain,
    ring, n_buf, rb_buf, h_buf, dg_buf, du_buf,
):
    length = second.shape[0]
    step = big_d
    ends = bounds(counts_d)
    _, start = big_plot(counts_d, ends, big_d)
    gain_row = gain[0:1, :].astype(F32)
    ready(cot)
    fill_rotation(ring, cot, length, step + 8)
    for r in range(0, length, step):
        rows = slice(r, r + step)
        c = rotated_rows(ring, wrap(r + start, length), step)
        grad_second[rows, :] = jnp.where(row_mask(start, ends, length, r, step), c, 0.0)
    total = None
    ready(second, gu, wd)
    for r in range(0, length, step):
        rows = slice(r, r + step)
        x = second[rows, :]
        c = grad_second[rows, :]
        h, gn = ffn_back_rows(x, gain_row, gu, wd, c, n_buf, rb_buf, h_buf, dg_buf, du_buf, rows)
        ring[rows, :] = x + dot(h, wd[...])
        gx, gg = norm_back(x, gain_row, gn)
        grad_second[rows, :] = c + gx
        total = gg if total is None else total + gg
    d_gain[...] = total
    store(grad_second)
    ready(wo2, mixed2)
    for r in range(0, length, step):
        rows = slice(r, r + step)
        go2[rows, :] = dot(grad_second[rows, :].astype(BF), wo2[...], NT).astype(BF)
    store(go2)
    put_back(ring, start, length, step + 8, step, out)
    store(out)
    places = ffn_weight_grads(coords[0], n_buf, rb_buf, h_buf, dg_buf, du_buf, send, keep)
    out_proj_grads(places, mixed2, grad_second)


def enc_ffn_kernel(
    big_e, coords, counts_e, mid, cot, grad_memory, gu, wd, gains, wo, mixed,
    grad_mid, go, send, keep, d_gain,
    ring, n_buf, rb_buf, h_buf, dg_buf, du_buf,
):
    length = mid.shape[0]
    step = length - big_e
    ends = bounds(counts_e)
    _, start = big_plot(counts_e, ends, big_e)
    gain_row = gains[1:2, :].astype(F32)
    ready(cot)
    fill_rotation(ring, cot, length, step + 8)
    total = None
    ready(mid, grad_memory, gu, wd)
    for r in range(0, length, step):
        rows = slice(r, r + step)
        c = rotated_rows(ring, wrap(r + start, length), step)
        c = jnp.where(row_mask(start, ends, length, r, step), c, 0.0) + grad_memory[rows, :]
        x = mid[rows, :]
        _, gn = ffn_back_rows(x, gain_row, gu, wd, c, n_buf, rb_buf, h_buf, dg_buf, du_buf, rows)
        gx, gg = norm_back(x, gain_row, gn)
        grad_mid[rows, :] = c + gx
        total = gg if total is None else total + gg
    d_gain[...] = total
    store(grad_mid)
    ready(wo, mixed)
    for r in range(0, length, step):
        rows = slice(r, r + step)
        go[rows, :] = dot(grad_mid[rows, :].astype(BF), wo[...], NT).astype(BF)
    store(go)
    places = ffn_weight_grads(coords[0], n_buf, rb_buf, h_buf, dg_buf, du_buf, send, keep)
    out_proj_grads(places, mixed, grad_mid)


def cross_pair_kernel(
    big_e, big_d, counts_e, counts_d, go, q, k, v, mixed, lse, dq, dk, dv, got, qt, dkt, dvt, bias
):
    length, length_e = q.shape[0], k.shape[0]
    ends_d, ends_e = bounds(counts_d), bounds(counts_e)
    index_d, start_d = big_plot(counts_d, ends_d, big_d)
    index_e, start_e = big_plot(counts_e, ends_e, big_e)
    transposes(q, go, qt, got, dkt, dvt)
    cross_setup(ends_d, start_d, big_d, length, index_e, start_e, ends_e, big_e, length_e, bias)
    seg_col = segments(iota((length - big_d, 1), 0) + big_d, start_d, ends_d, length)
    col = lambda: jnp.where(seg_col == index_e, 0.0, NEG)

    def run(rows, parts):
        attend_back(q, qt, go, got, mixed, lse, rows, parts, dq, dkt, dvt, q.shape[1] // 128)

    cross_run(index_d == index_e, big_d, length, big_e, length_e, col, bias, k, v, run)
    turn_back(dkt, dvt, dk, dv)


def transposes(q, go, qt, got, dkt, dvt):
    for r in range(0, q.shape[0], 512):
        qt[:, r : r + 512] = q[r : r + 512, :].T
        got[:, r : r + 512] = go[r : r + 512, :].T
    dkt[...] = jnp.zeros_like(dkt)
    dvt[...] = jnp.zeros_like(dvt)


def turn_back(dkt, dvt, dk, dv):
    for r in range(0, dk.shape[0], 512):
        dk[r : r + 512, :] = dkt[:, r : r + 512].T.astype(BF)
        dv[r : r + 512, :] = dvt[:, r : r + 512].T.astype(BF)


def joined(blocks):
    return jnp.concatenate([b[...] for b in blocks], axis=1)


def cross_tail_kernel(
    coords, grad_second, after, memory, dq0, dq1, dq2, dk0, dk1, dk2, dv0, dv1, dv2, qkv, gains, wo1, mixed1,
    grad_first, grad_memory, go1, send, keep, d_gain, dq, dk, dv, n_buf, rb,
):
    step = 512
    gain_row = gains[1:2, :].astype(F32)
    ready(dq0, dq1, dq2, dk0, dk1, dk2, dv0, dv1, dv2, qkv)
    for i, (a, b, c) in enumerate(((dq0, dk0, dv0), (dq1, dk1, dv1), (dq2, dk2, dv2))):
        sl = slice(i * LANES, (i + 1) * LANES)
        dq[:, sl] = a[...]
        dk[:, sl] = b[...]
        dv[:, sl] = c[...]
    for r in range(0, memory.shape[0], step):
        rows = slice(r, r + step)
        grad_memory[rows, :] = dot(dk[rows, :], qkv[1], NT) + dot(dv[rows, :], qkv[2], NT)
    store(grad_memory)
    ready(grad_second, after, wo1, memory, mixed1)
    total = None
    for r in range(0, after.shape[0], step):
        rows = slice(r, r + step)
        x = after[rows, :]
        n_buf[rows, :] = (x * inverse_rms(x) * gain_row).astype(BF)
        gx, gg = norm_back(x, gain_row, dot(dq[rows, :], qkv[0], NT))
        g = grad_second[rows, :] + gx
        grad_first[rows, :] = g
        rb[rows, :] = g.astype(BF)
        go1[rows, :] = dot(rb[rows, :], wo1[...], NT).astype(BF)
        total = gg if total is None else total + gg
    d_gain[...] = total
    store(grad_first, go1)
    out_proj_grads(qkv_grads(coords[0], n_buf, memory, dq, dk, dv, send, keep), mixed1, rb)


def self_tail(core, step, grad, xr, qkv, gain_row, start, dq, dk, dv, n_buf, ring, send, keep, out, later=False):
    total = None
    ready(grad, xr, qkv)
    length = xr.shape[0]
    for r in range(0, length, step):
        rows = slice(r, r + step)
        x = xr[rows, :].astype(F32)
        n_buf[rows, :] = (x * inverse_rms(x) * gain_row).astype(BF)
        gn = dot(dq[rows, :], qkv[0], NT) + dot(dk[rows, :], qkv[1], NT) + dot(dv[rows, :], qkv[2], NT)
        gx, gg = norm_back(x, gain_row, gn)
        ring[rows, :] = grad[rows, :] + gx
        total = gg if total is None else total + gg
    put_back(ring, start, length, step + 8, step, out)
    store(out)
    for ref, _, _ in qkv_grads(core, n_buf, n_buf, dq, dk, dv, send, keep):
        if not later:
            store(ref)
    return total


def dec_self_back_kernel(
    big_d,
    coords, counts_d, go, grad_first, xr, q, k, v, mixed, lse, qkv, gains,
    out, send, keep, d_gain,
    ring, got, qt, dq, dkt, dvt, dk, dv, n_buf, bias,
):
    length = xr.shape[0]
    ends = bounds(counts_d)
    _, start = big_plot(counts_d, ends, big_d)
    ready(q, go, k, v, mixed, lse)
    transposes(q, go, qt, got, dkt, dvt)
    self_bias(bias, big_d, start, ends, length)
    for rows, parts in self_tiles(big_d, bias, k, v):
        attend_back(q, qt, go, got, mixed, lse, rows, parts, dq, dkt, dvt, q.shape[1] // 128)
    turn_back(dkt, dvt, dk, dv)
    d_gain[...] = self_tail(
        coords[0], big_d, grad_first, xr, qkv, gains[0:1, :].astype(F32), start,
        dq, dk, dv, n_buf, ring, send, keep, out,
    )


def enc_pair_kernel(big_e, counts_e, go, q, k, v, mixed, lse, dq, dk, dv, got, qt, dkt, dvt, bias):
    length = q.shape[0]
    rest = length - big_e
    ends = bounds(counts_e)
    _, start = big_plot(counts_e, ends, big_e)
    transposes(q, go, qt, got, dkt, dvt)
    sq = segments(iota((rest, rest), 0) + big_e, start, ends, length)
    sk = segments(iota((rest, rest), 1) + big_e, start, ends, length)
    bias[...] = jnp.where(sq == sk, 0.0, NEG)
    pairs = q.shape[1] // 128
    for r in range(0, big_e, rest):
        attend_back(q, qt, go, got, mixed, lse, (r, r + rest), [(k, v, 0, big_e, None)], dq, dkt, dvt, pairs)
    parts = [(k, v, big_e, length, lambda: bias[...])]
    attend_back(q, qt, go, got, mixed, lse, (big_e, length), parts, dq, dkt, dvt, pairs)
    turn_back(dkt, dvt, dk, dv)


def enc_tail_kernel(
    big_e,
    coords, counts_e, grad_mid, xr, dq0, dq1, dq2, dk0, dk1, dk2, dv0, dv1, dv2, qkv, gains,
    gain_e2, gain_d1, gain_d2, gain_d3,
    out, send, keep, ring, dq, dk, dv, n_buf,
):
    rest = xr.shape[0] - big_e
    _, start = big_plot(counts_e, bounds(counts_e), big_e)
    ready(dq0, dq1, dq2, dk0, dk1, dk2, dv0, dv1, dv2)
    for i, (a, b, c) in enumerate(((dq0, dk0, dv0), (dq1, dk1, dv1), (dq2, dk2, dv2))):
        sl = slice(i * LANES, (i + 1) * LANES)
        dq[:, sl] = a[...]
        dk[:, sl] = b[...]
        dv[:, sl] = c[...]
    gain_e1 = self_tail(
        coords[0], rest, grad_mid, xr, qkv, gains[0:1, :].astype(F32), start, dq, dk, dv, n_buf, ring, send, keep, out, True
    )
    rows = []
    for gain in (gain_e1, gain_e2[...], gain_d1[...], gain_d2[...], gain_d3[...]):
        rows += [gain[:, j : j + LANES] for j in range(0, gain.shape[1], LANES)]
    at = keep.shape[0] - EXTRA
    for ref in (send, keep):
        ref[at:, :] = jnp.zeros((EXTRA, LANES), F32)
        for i, row in enumerate(rows):
            ref[at + i : at + i + 1, :] = row


LANES = 128


def pairs_of(size, bit):
    return [(i, i ^ bit) for i in range(size)]


def turns_of(size, unit, count, by):
    out = []
    for i in range(size):
        place = (i // unit) % count
        out.append((i, i + ((place + by) % count - place) * unit))
    return out


def step_kernel(n_in, jobs, coords, *refs):
    where = tuple(coords[i] for i in range(4))
    ins, outs = refs[:n_in], refs[n_in:]
    for out, at, rows, terms in jobs:
        chunk = next(c for c in (512, 384, 256, 192, 128, 96, 64, 48, 32, 24, 16, 8) if rows % c == 0)
        to = at(where) if callable(at) else at
        froms = [(i, off(where) if callable(off) else off) for i, off in terms]

        def one(j, carry, out=out, to=to, froms=froms, chunk=chunk):
            def place(base):
                return pl.ds(pl.multiple_of(base + j * chunk, 8), chunk)

            total = ins[froms[0][0]][place(froms[0][1]), :]
            for i, off in froms[1:]:
                total = total + ins[i][place(off), :]
            outs[out][place(to), :] = total
            return carry

        lax.fori_loop(0, rows // chunk, one, 0)


STREAMED = (
    "enc_forward", "dec_forward", "dec_ffn", "enc_ffn",
)


class Stream:
    now = None

    def __init__(self):
        self.coming, self.going, self.left = {}, {}, []

    def finish(self):
        for copy in self.coming.values():
            copy.wait()
        for copy in self.going.values():
            copy.start()
        for copy in self.left + list(self.going.values()):
            copy.wait()


def ready(*refs):
    for ref in refs:
        copy = Stream.now and Stream.now.coming.pop(id(ref), None)
        if copy is not None:
            copy.wait()


def store(*refs):
    for ref in refs:
        copy = Stream.now and Stream.now.going.pop(id(ref), None)
        if copy is not None:
            copy.start()
            Stream.now.left.append(copy)


class Chain:
    def __init__(self):
        self.last = None

    def __call__(self, kernel, name, scalars, arrays, outs, scratch, flops, limit, blocks=None):
        vmem = pl.BlockSpec(memory_space=pltpu.VMEM)
        smem = pl.BlockSpec(memory_space=pltpu.SMEM)
        before = [] if self.last is None else [self.last]
        size = sum(a.size * a.dtype.itemsize for a in (*arrays, *outs))
        count = len(scalars) + len(arrays)

        big = lambda a: not blocks and outs and name in STREAMED and a.size * a.dtype.itemsize >= 1 << 18
        moved_in = [i for i, a in enumerate(arrays) if big(a)]
        moved_out = [i for i, o in enumerate(outs) if big(o)]
        copies = len(moved_in) + len(moved_out)

        def body(*refs):
            given, rest = list(refs[:count]), list(refs[count + len(before) :])
            if not copies:
                return kernel(*given, *rest)
            own, sems = rest[-copies - 1 : -1], rest[-1]
            rest = rest[: -copies - 1]
            stream = Stream()
            for n, i in enumerate(moved_in):
                copy = pltpu.make_async_copy(given[len(scalars) + i], own[n], sems.at[n])
                copy.start()
                given[len(scalars) + i] = own[n]
                stream.coming[id(own[n])] = copy
            for n, i in enumerate(moved_out, len(moved_in)):
                stream.going[id(own[n])] = pltpu.make_async_copy(own[n], rest[i], sems.at[n])
                rest[i] = own[n]
            Stream.now = stream
            kernel(*given, *rest)
            stream.finish()
            Stream.now = None

        specs = [vmem] * len(arrays)
        out_specs = [vmem] * len(outs)
        for i in moved_in:
            specs[i] = pl.BlockSpec(memory_space=pl.ANY)
        for i in moved_out:
            out_specs[i] = pl.BlockSpec(memory_space=pl.ANY)
        kept = [pltpu.VMEM(arrays[i].shape, arrays[i].dtype) for i in moved_in]
        kept += [pltpu.VMEM(outs[i].shape, outs[i].dtype) for i in moved_out]
        kept += [pltpu.SemaphoreType.DMA((copies,))] if copies else []
        for i, spec in (blocks or {}).items():
            specs[i] = spec
        got = pl.pallas_call(
            body,
            out_shape=tuple(outs),
            in_specs=[smem] * len(scalars) + specs + [pl.BlockSpec(memory_space=pl.ANY)] * len(before),
            out_specs=tuple(out_specs),
            scratch_shapes=[pltpu.VMEM(s, d) for s, d in scratch] + kept,
            compiler_params=pltpu.CompilerParams(vmem_limit_bytes=limit),
            cost_estimate=pl.CostEstimate(flops=0 if name in SHORT else flops * HINT, bytes_accessed=0, transcendentals=0),
            name=name,
            **({"grid": (1,)} if blocks else {}),
        )(*scalars, *arrays, *before)
        self.last = min(got, key=lambda o: o.size * o.dtype.itemsize)
        return got


def run_step(chain, name, coords, arrays, out_rows, jobs):
    moved = 4 * LANES * (sum(a.shape[0] for a in arrays) + sum(out_rows))
    outs = [jax.ShapeDtypeStruct((r, LANES), F32) for r in out_rows]
    kernel = functools.partial(step_kernel, len(arrays), jobs)
    return chain(kernel, name, [coords], arrays, outs, [], 0, moved + (2 << 20))


def swap(v, first):
    dp, batch = lax.axis_size("dp"), lax.axis_size("batch")
    out = []
    for i in range(dp):
        for j in range(batch):
            along_x = (i % 2 == 0) == first
            out.append((i * batch + j, (i ^ 2) * batch + j if along_x else i * batch + (j ^ 1)))
    return lax.ppermute(v, AXES, out)


def core_swap(v):
    return lax.ppermute(v, "dp", pairs_of(lax.axis_size("dp"), 1))


def z_send(v, by):
    return lax.ppermute(v, "dp", turns_of(lax.axis_size("dp"), 4, 4, by))


def over_rest(values):
    size = lax.axis_size("dp")
    if size == 16:
        return values
    groups = [list(range(i, size, 16)) for i in range(16)]
    return [lax.psum(v, "dp", axis_index_groups=groups) for v in values]


def reduce_gather(chain, coords, send, keep, extra, tag, whole=False):
    h = keep.shape[0] - extra
    got = core_swap(send)
    rows, now = h, [keep, got]
    for level in (1, 2):
        yield
        rows //= 2
        mine = lambda w, level=level, rows=rows: w[level] * rows
        theirs = lambda w, level=level, rows=rows: (1 - w[level]) * rows
        jobs = [(0, 0, rows, [(0, theirs), (1, theirs)]), (1, 0, rows, [(0, mine), (1, mine)])]
        if extra:
            jobs += [(o, rows, extra, [(0, 2 * rows), (1, 2 * rows)]) for o in (0, 1)]
        out, kept = run_step(chain, f"sum{level}_{tag}", coords, now, [rows + extra] * 2, jobs)
        now = [kept, swap(out, level == 1)]
    yield
    e, p = rows, rows // 4
    jobs = []
    for d in range(4):
        off = lambda w, d=d: ((w[3] + d) % 4) * p
        jobs.append((d, 0, p, [(0, off), (1, off)]))
        if extra:
            jobs.append((d, p, extra, [(0, e), (1, e)]))
    parts = run_step(chain, f"sum3_{tag}", coords, now, [p + extra] * 4, jobs)
    parts = [parts[0]] + [z_send(parts[d], d) for d in (1, 2, 3)]
    yield
    jobs = [(0, 0, p, [(i, 0) for i in range(4)])]
    if extra:
        jobs.append((1, 0, extra, [(i, p) for i in range(4)]))
    done = over_rest(run_step(chain, f"sum4_{tag}", coords, parts, [p] + [extra] * (extra > 0), jobs))
    own, total = done[0], (done[1] if extra else None)
    if whole:
        every = lax.all_gather(own, AXES, axis=0, tiled=True)
        yield
        return every, None, total
    parts = [own] + [z_send(own, d) for d in (1, 2, 3)]
    yield
    jobs = [(0, lambda w, d=d: ((w[3] + 4 - d) % 4) * p, p, [(d, 0)]) for d in range(4)]
    (part,) = run_step(chain, f"put5_{tag}", coords, parts, [e], jobs)
    for level in (2, 1):
        other = swap(part, level == 1)
        yield
        mine = lambda w, level=level, rows=rows: w[level] * rows
        theirs = lambda w, level=level, rows=rows: (1 - w[level]) * rows
        jobs = [(0, mine, rows, [(0, 0)]), (0, theirs, rows, [(1, 0)])]
        rows *= 2
        (part,) = run_step(chain, f"put{8 - level}_{tag}", coords, [part, other], [rows], jobs)
    other = core_swap(part)
    yield
    return part, other, total


def coords_of():
    dp, y = lax.axis_index("dp"), lax.axis_index("batch")
    core, x = dp % 2, (dp // 2) % 2
    first, second = jnp.where(core == 0, x, y), jnp.where(core == 0, y, x)
    return jnp.stack([core, first, second, (dp // 4) % 4]).astype(jnp.int32)


def like(shape, dtype):
    return jax.ShapeDtypeStruct(shape, dtype)


class Group:
    def __init__(self, chain, coords, pair, extra, outs, tag, whole=False):
        self.chain, self.coords, self.outs, self.tag = chain, coords, outs, tag
        self.whole = whole and lax.axis_size("dp") == 16
        self.work = reduce_gather(chain, coords, *pair, extra, tag, self.whole)
        self.result = None
        next(self.work)

    def step(self):
        try:
            next(self.work)
        except StopIteration as end:
            own, other, self.total = end.value
            size = 8 * sum(o.size for o in self.outs)
            if self.whole:
                self.result = self.chain(
                    spread_kernel, f"final_{self.tag}", [], [own], self.outs, [], 0, size + (4 << 20)
                )
                return
            self.result = self.chain(
                final_kernel, f"final_{self.tag}", [self.coords], [own, other], self.outs, [], 0, size + (4 << 20)
            )


def shards(
    enc_input, dec_input, patch_counts, table_lengths,
    enc_qkv, enc_wo, enc_gu, enc_wd, enc_gains,
    self_qkv, self_wo, cross_qkv, cross_wo, dec_gu, dec_wd, dec_gains, dec_gain, enc_cot, dec_cot,
):
    chain = Chain()
    coords = coords_of()
    le, width = enc_input.shape[1:]
    ld = dec_input.shape[1]
    inner = enc_wo.shape[0]
    ff = enc_wd.shape[0]
    big_e, big_d = le - le // 4, ld // 2
    rest_e = le - big_e
    enc_row, dec_row, counts, lengths = enc_input[0], dec_input[0], patch_counts, table_lengths
    limit = 58 << 20
    third = lambda i: pl.BlockSpec((le, LANES), lambda _: (0, i))
    third_d = lambda i: pl.BlockSpec((ld, LANES), lambda _: (0, i))
    groups = {}

    out_e, memory, xr_e, q_e, k_e, v_e, mixed_e, lse_e, mid = chain(
        functools.partial(enc_forward_kernel, big_e), "enc_forward",
        [counts], [enc_row, enc_qkv, enc_wo, enc_gu, enc_wd, enc_gains],
        [like((le, width), BF)] * 3 + [like((le, inner), BF)] * 4 + [like((le, inner), F32), like((le, width), F32)],
        [((le + rest_e + 8, width), F32), ((rest_e, rest_e), F32)], 11_000_000_000, limit,
    )
    xr_d, q1, k1, v1, mixed1, lse1, after, q2, k2, v2, mixed2, lse2, second = chain(
        functools.partial(dec_forward_kernel, big_e, big_d), "dec_forward",
        [counts, lengths], [dec_row, memory, self_qkv, self_wo, cross_qkv, cross_wo, dec_gains],
        [like((ld, width), BF)] + [like((ld, inner), BF)] * 4 + [like((ld, inner), F32), like((ld, width), F32)]
        + [like((ld, inner), BF), like((le, inner), BF), like((le, inner), BF), like((ld, inner), BF)]
        + [like((ld, inner), F32), like((ld, width), F32)],
        [((ld + big_d + 8, width), F32), ((2, big_d, big_d), F32), ((2, ld - big_d, rest_e), F32)],
        8_000_000_000, limit,
    )

    def ffn_scratch(length, extra):
        return [((length + extra + 8, width), F32), ((length, width), BF), ((length, width), BF)] + [((length, ff), BF)] * 3

    def pair_scratch(lq, lk):
        return [((LANES, lq), BF), ((LANES, lq), BF), ((LANES, lk), F32), ((LANES, lk), F32)]

    def grads(*sizes, extra=0):
        return [like((sum(sizes) // 2 // LANES + extra, LANES), F32)] * 2

    ffn_size, qkv_size, wo_size = 3 * width * ff, 3 * width * inner, inner * width
    ffn_outs = [like((2, width, ff), F32), like((ff, width), F32), like((inner, width), F32)]
    qkv_outs = [like((3, width, inner), F32)]
    wo_outs = [like((inner, width), F32)]
    gain_out = [like((1, width), F32)]

    out_d, grad_second, go2, *sums, d_gain3 = chain(
        functools.partial(dec_ffn_kernel, big_d), "dec_ffn",
        [coords, lengths], [second, dec_cot[0], dec_gu, dec_wd, dec_gain.reshape(1, width), cross_wo, mixed2],
        [like((ld, width), BF), like((ld, width), F32), like((ld, inner), BF)] + grads(ffn_size, wo_size) + gain_out,
        ffn_scratch(ld, big_d), 10_000_000_000, limit,
    )
    groups[1] = Group(chain, coords, sums, 0, ffn_outs, "dec_ffn", True)

    def advance(*numbers):
        for number in numbers:
            if groups[number].result is None:
                groups[number].step()

    blocks = []
    for i in range(3):
        blocks.append(
            chain(
                functools.partial(cross_pair_kernel, big_e, big_d), f"cross_pair{i}",
                [counts, lengths], [go2, q2, k2, v2, mixed2, lse2],
                [like((ld, LANES), BF), like((le, LANES), BF), like((le, LANES), BF)],
                pair_scratch(ld, le) + [((2, ld - big_d, rest_e), F32)], 4_000_000_000, PAIR_LIMIT,
                {0: third_d(i), 1: third_d(i), 2: third(i), 3: third(i), 4: third_d(i), 5: third_d(i)},
            )
        )
        advance(*PLAN["cross", i])
    dq, dk, dv = zip(*blocks)
    grad_first, grad_memory, go1, *sums, d_gain2 = chain(
        cross_tail_kernel, "cross_tail",
        [coords], [grad_second, after, memory, *dq, *dk, *dv, cross_qkv, dec_gains, self_wo, mixed1],
        [like((ld, width), F32), like((le, width), F32), like((ld, inner), BF)] + grads(qkv_size, wo_size) + gain_out,
        [((ld, inner), BF), ((le, inner), BF), ((le, inner), BF), ((ld, width), BF), ((ld, width), BF)],
        4_000_000_000, limit,
    )
    groups[2] = Group(chain, coords, sums, 0, qkv_outs + wo_outs, "cross")
    advance(*PLAN["cross_tail"])
    grad_mid, go_e, *sums, d_enc_gain2 = chain(
        functools.partial(enc_ffn_kernel, big_e), "enc_ffn",
        [coords, counts], [mid, enc_cot[0], grad_memory, enc_gu, enc_wd, enc_gains, enc_wo, mixed_e],
        [like((le, width), F32), like((le, inner), BF)] + grads(ffn_size, wo_size) + gain_out,
        ffn_scratch(le, rest_e), 14_000_000_000, limit,
    )
    groups[3] = Group(chain, coords, sums, 0, ffn_outs, "enc_ffn")
    advance(*PLAN["enc_ffn"])
    grad_dec, *sums, d_gain1 = chain(
        functools.partial(dec_self_back_kernel, big_d), "dec_self_back",
        [coords, lengths], [go1, grad_first, xr_d, q1, k1, v1, mixed1, lse1, self_qkv, dec_gains],
        [like((ld, width), F32)] + grads(qkv_size) + gain_out,
        [
            ((ld + big_d + 8, width), F32), ((inner, ld), BF), ((inner, ld), BF), ((ld, inner), BF),
            ((inner, ld), F32), ((inner, ld), F32), ((ld, inner), BF), ((ld, inner), BF), ((ld, width), BF),
            ((2, big_d, big_d), F32),
        ],
        6_000_000_000, limit,
    )
    groups[4] = Group(chain, coords, sums, 0, qkv_outs, "dec_self")
    advance(*PLAN["dec_self"])
    blocks = []
    for i in range(3):
        blocks.append(
            chain(
                functools.partial(enc_pair_kernel, big_e), f"enc_pair{i}",
                [counts], [go_e, q_e, k_e, v_e, mixed_e, lse_e],
                [like((le, LANES), BF)] * 3,
                pair_scratch(le, le) + [((rest_e, rest_e), F32)], 5_000_000_000, PAIR_LIMIT,
                {j: third(i) for j in range(6)},
            )
        )
        advance(*PLAN["enc", i])
    dq, dk, dv = zip(*blocks)
    grad_enc, *sums = chain(
        functools.partial(enc_tail_kernel, big_e), "enc_tail",
        [coords, counts],
        [grad_mid, xr_e, *dq, *dk, *dv, enc_qkv, enc_gains, d_enc_gain2, d_gain1, d_gain2, d_gain3],
        [like((le, width), F32)] + grads(qkv_size, extra=EXTRA),
        [((le + rest_e + 8, width), F32)] + [((le, inner), BF)] * 3 + [((le, width), BF)],
        6_000_000_000, limit,
    )
    groups[5] = Group(chain, coords, sums, EXTRA, qkv_outs, "enc_self")
    advance(*PLAN["enc_tail"])
    while any(group.result is None for group in groups.values()):
        advance(*TAIL)

    d_dec_gu, d_dec_wd, d_cross_wo = groups[1].result
    d_cross_qkv, d_self_wo = groups[2].result
    d_enc_gu, d_enc_wd, d_enc_wo = groups[3].result
    (d_self_qkv,) = groups[4].result
    (d_enc_qkv,) = groups[5].result
    gains = groups[5].total[: 5 * width // LANES].reshape(5, width)
    return (
        out_e[None], out_d[None], grad_enc[None], grad_dec[None],
        d_enc_qkv, d_enc_wo, d_enc_gu, d_enc_wd, gains[0:2],
        d_self_qkv, d_self_wo, d_cross_qkv, d_cross_wo, d_dec_gu, d_dec_wd, gains[2:4], gains[4],
    )


HINT = 20
SHORT = ('cross_pair2', 'cross_tail', 'enc_tail')
PAIR_LIMIT = 40 << 20
PLAN = {
    ("cross", 0): (1,),
    ("cross", 1): (),
    ("cross", 2): (),
    "cross_tail": (1,),
    "enc_ffn": (1, 2),
    "dec_self": (1, 2, 3),
    ("enc", 0): (2, 4),
    ("enc", 1): (3, 2),
    ("enc", 2): (4, 3, 2),
    "enc_tail": (),
}
TAIL = (5, 3, 4, 5, 2, 3, 4, 5, 3, 4, 2, 5, 3, 4, 5, 2, 1, 5, 4, 3, 5, 4, 5)


def solution(mesh):
    rows3 = P(AXES, None, None)
    rows2 = P(AXES, None)
    return jax.shard_map(
        shards,
        mesh=mesh,
        in_specs=(rows3, rows3, rows2, rows2) + (P(),) * 13 + (rows3, rows3),
        out_specs=(rows3,) * 4 + (P(),) * 13,
        check_vma=False,
    )
```
